128 devices in a mesh: group: 4 (over y), table: 32 (over x, z, core).
Axes of the slice: x: 4, y: 4, z: 4, core: 2. Of those that a mesh axis runs over, the one named last changes fastest.
Arguments:
- user_vec: bfloat16 [16384, 256], P(('group', 'table')), may hold values from -12 to 12
- cluster_rows: bfloat16 [65536, 256], P(('group', 'table')), may hold values from -0.5625 to 0.5625
- leaf_rows: bfloat16 [256, 4096, 256], P(('group', 'table')), may hold values from -0.5625 to 0.5625
- touched: int32 [256], P(('group', 'table')), may hold values from 0 to 511, as said below
- route_owner: int32 [16384], P(('group', 'table')), may hold values from 0 to 127, as said below
- route_slot: int32 [16384], P(('group', 'table')), may hold values from 0 to 1
- leaf_label: int32 [16384], P(('group', 'table')), may hold values from 0 to 4095
Outputs:
- user_grad: float32 [16384, 256], P(('group', 'table'))
- cluster_grad: float32 [65536, 256], P(('group', 'table'))
- leaf_grad: bfloat16 [256, 4096, 256], P(('group', 'table'))
The draws below stay inside these ranges and needn't reach their ends.
Inputs may be any that keep to these rules, and one draw needn't show every extreme that they name: `touched`: the 2 entries of one owner are distinct local cluster indices. `route_owner`: among the 128 users of one device at most 2 name the same owner, and one owner is named by 2 users of every device.
All inputs are finite; a program needn't handle non-finite values.
Results may differ from the reference program's by a relative error of at most 0.0034.
Values may be sent and summed in bfloat16 or wider, within the bound.
No kernel may reach another device: no remote copies, remote signals or barrier semaphores. Data moves between devices by JAX's collectives and lax.ppermute only.
A program may use at most 192 MiB of HBM per device.

```python
import math
import jax
import jax.numpy as jnp
from jax import lax

E = 256
LEAVES = 4096
CL_DEV = 512
TOUCH = 2
B_DEV = 128
OWNERS = 128
USERS = 16384
CLUSTERS = 65536
CAP = 2


def align_signs(key):
    return jax.random.bernoulli(key, 0.5, (E,)).astype(jnp.float32) * 2.0 - 1.0


def drawn_rows(key, shape, sign_vec, local_ids):
    jitter = jax.random.uniform(key, shape, jnp.float32, -0.1, 0.1)
    shared = jnp.mean(jitter * sign_vec, axis=-1, keepdims=True)
    jitter = jitter - shared * sign_vec
    return 0.4 * sign_vec + 0.2 / E * local_ids * sign_vec + jitter


def table_values(key, shape):
    root = 1.0 / math.sqrt(E)
    values = jax.random.uniform(key, shape, jnp.float32, -5.12 * root, 5.12 * root)
    return values


def draw_user_vec(key, part):
    sign_vec = align_signs(key)
    key = jax.random.fold_in(key, 3)
    normal_key = jax.random.fold_in(key, 0)
    normals = jnp.clip(jax.random.normal(normal_key, (USERS, E), jnp.float32), -4.0, 4.0)
    values = normals
    row_ids = jnp.arange(USERS)
    strong = row_ids % 61 == 0
    strength = 8.0 + 2.0 * (row_ids // 61 % 3).astype(jnp.float32)
    values = jnp.where(strong[:, None], sign_vec[None, :] * strength[:, None], values)
    return values.astype(jnp.bfloat16)


def draw_cluster_rows(key, part):
    sign_vec = align_signs(key)
    key = jax.random.fold_in(key, 4)
    normal_key, jitter_key = jax.random.split(key)
    values = table_values(normal_key, (CLUSTERS, E))
    local_ids = (jnp.arange(CLUSTERS) % CL_DEV).astype(jnp.float32)[:, None]
    aligned = drawn_rows(jitter_key, (CLUSTERS, E), sign_vec, local_ids)
    values = jnp.where(local_ids < 4.0, aligned, values)
    return values.astype(jnp.bfloat16)


def draw_leaf_rows(key, part):
    sign_vec = align_signs(key)
    key = jax.random.fold_in(key, 7)
    shape = (OWNERS * TOUCH, LEAVES, E)
    normal_key, jitter_key = jax.random.split(key)
    values = table_values(normal_key, shape)
    local_ids = jnp.arange(LEAVES).astype(jnp.float32)[None, :, None]
    aligned = drawn_rows(jitter_key, shape, sign_vec, local_ids)
    values = jnp.where(local_ids < 4.0, aligned, values)
    return values.astype(jnp.bfloat16)


def draw_touched(key, part):
    key = jax.random.fold_in(key, 5)
    hot_key, owner_key = jax.random.split(key)
    special = jax.random.randint(hot_key, (), 0, OWNERS)

    def one_owner(owner_id):
        key_off, key_step = jax.random.split(jax.random.fold_in(owner_key, owner_id))
        offset = jax.random.randint(key_off, (), 0, CL_DEV)
        stride = jax.random.randint(key_step, (), 1, CL_DEV // TOUCH)
        offset = jnp.where(owner_id == special, CL_DEV - 1, offset)
        stride = jnp.where(owner_id == special, 1, stride)
        return (offset + jnp.arange(TOUCH) * stride) % CL_DEV
    return jax.vmap(one_owner)(jnp.arange(OWNERS)).reshape(-1).astype(jnp.int32)


def draw_route_owner(key, part):
    key = jax.random.fold_in(key, 6)
    hot_key, source_key = jax.random.split(key)
    hot_owner = jax.random.randint(hot_key, (), 0, OWNERS)
    slot_total = OWNERS * CAP

    def one_source(source_id):
        key_rank, key_shuffle = jax.random.split(jax.random.fold_in(source_key, source_id))
        slot_ids = jnp.arange(slot_total)
        ranking = jax.random.randint(key_rank, (slot_total,), 0, 2 ** 20) * slot_total + slot_ids
        ranking = jnp.where(slot_ids // CAP == hot_owner, 2 ** 30 + slot_ids, ranking)
        picked = lax.top_k(ranking, B_DEV)[1]
        owner_ids = picked // CAP
        shuffle = jax.random.permutation(key_shuffle, B_DEV)
        return owner_ids[shuffle]
    return jax.vmap(one_source)(jnp.arange(OWNERS)).reshape(-1).astype(jnp.int32)


def with_ends(drawn, own_key, smallest, largest):
    spot = [jax.random.randint(jax.random.fold_in(own_key, axis), (), 0, length) for axis, length in enumerate(drawn.shape)]
    longest = drawn.shape.index(max(drawn.shape))
    next_to = spot[:longest] + [(spot[longest] + 1) % drawn.shape[longest]] + spot[longest + 1:]
    return drawn.at[tuple(spot)].set(smallest).at[tuple(next_to)].set(largest)


def setup_inputs(seed: int = 0) -> dict:
    seeds = jax.random.split(jax.random.key(seed), 8)
    return {
        "user_vec": draw_user_vec(jax.random.fold_in(seeds[7], 71), 0),
        "cluster_rows": draw_cluster_rows(jax.random.fold_in(seeds[7], 71), 0),
        "leaf_rows": draw_leaf_rows(jax.random.fold_in(seeds[7], 71), 0),
        "touched": draw_touched(jax.random.fold_in(seeds[7], 71), 0),
        "route_owner": draw_route_owner(jax.random.fold_in(seeds[7], 71), 0),
        "route_slot": with_ends(jax.random.randint(seeds[5], (USERS,), 0, TOUCH), jax.random.fold_in(seeds[5], 1), 0, TOUCH - 1).astype(jnp.int32),
        "leaf_label": with_ends(jax.random.randint(seeds[6], (USERS,), 0, LEAVES), jax.random.fold_in(seeds[6], 1), 0, LEAVES - 1).astype(jnp.int32),
    }


def leaf_terms(owner_users, owner_slots, owner_leaves, is_live, owner_tables):
    users_wide = owner_users.astype(jnp.float32)
    targets = (owner_leaves[:, None] == jnp.arange(LEAVES)[None, :]).astype(jnp.float32)
    user_part = jnp.zeros(users_wide.shape, jnp.float32)
    table_parts = []
    for table_index in range(TOUCH):
        table_wide = owner_tables[table_index].astype(jnp.float32)
        scores = jnp.dot(users_wide, table_wide.T, preferred_element_type=jnp.float32)
        peak = jnp.max(scores, axis=1, keepdims=True)
        weights = jnp.exp(scores - peak)
        weights = weights / jnp.sum(weights, axis=1, keepdims=True)
        chosen = ((owner_slots == table_index) & is_live).astype(jnp.float32)[:, None]
        coeffs = ((weights - targets) * chosen).astype(jnp.bfloat16)
        coeffs = lax.optimization_barrier(coeffs).astype(jnp.float32)
        user_part = user_part + jnp.dot(coeffs, table_wide, preferred_element_type=jnp.float32)
        table_parts.append(jnp.dot(coeffs.T, users_wide, preferred_element_type=jnp.float32))
    return user_part, jnp.stack(table_parts)


def reference(user_vec, cluster_rows, leaf_rows, touched, route_owner, route_slot, leaf_label):
    user_total = user_vec.shape[0]
    slot_total = OWNERS * CAP
    table_of = (route_owner * TOUCH + route_slot).astype(jnp.int32)
    label_cluster = (route_owner * CL_DEV + touched[table_of]).astype(jnp.int32)
    users_wide = user_vec.astype(jnp.float32)
    clusters_wide = cluster_rows.astype(jnp.float32)
    block_len = math.gcd(user_total, 512)

    def cluster_step(carry, user_block):
        scores = jnp.dot(user_block, clusters_wide.T, preferred_element_type=jnp.float32)
        peak = jnp.max(scores, axis=1, keepdims=True)
        log_total = peak + jnp.log(jnp.sum(jnp.exp(scores - peak), axis=1, keepdims=True))
        probs_bf = jnp.exp(scores - log_total).astype(jnp.bfloat16)
        probs_wide = lax.optimization_barrier(probs_bf).astype(jnp.float32)
        term = jnp.dot(probs_wide, clusters_wide, preferred_element_type=jnp.float32)
        carry = carry + jnp.dot(probs_wide.T, user_block, preferred_element_type=jnp.float32)
        return carry, term

    user_blocks = users_wide.reshape(user_total // block_len, block_len, E)
    prob_sums, cluster_terms = lax.scan(cluster_step, jnp.zeros((CLUSTERS, E), jnp.float32), user_blocks)
    cluster_terms = cluster_terms.reshape(user_total, E)

    sort_keys = (route_owner * user_total + jnp.arange(user_total)).astype(jnp.int32)
    sorted_ids = jnp.argsort(sort_keys).astype(jnp.int32)
    counts = jnp.sum((route_owner[None, :] == jnp.arange(OWNERS)[:, None]).astype(jnp.int32), axis=1)
    starts = (jnp.cumsum(counts) - counts).astype(jnp.int32)
    padded = jnp.concatenate([sorted_ids, jnp.zeros((slot_total,), jnp.int32)])

    def one_owner(owner_id):
        picked = lax.dynamic_slice(padded, (starts[owner_id].astype(jnp.int32),), (slot_total,))
        is_live = jnp.arange(slot_total) < counts[owner_id]
        owner_tables = lax.dynamic_slice_in_dim(leaf_rows, (owner_id * TOUCH).astype(jnp.int32), TOUCH, 0)
        user_part, table_parts = leaf_terms(user_vec[picked], route_slot[picked], leaf_label[picked], is_live, owner_tables)
        return picked, user_part, table_parts

    picked_all, leaf_users, leaf_parts = lax.map(one_owner, jnp.arange(OWNERS, dtype=jnp.int32))
    leaf_term = jnp.zeros((user_total, E), jnp.float32).at[picked_all.reshape(-1)].add(leaf_users.reshape(-1, E))
    user_grad = cluster_terms - clusters_wide[label_cluster] + leaf_term
    label_sums = jnp.zeros((CLUSTERS, E), jnp.float32).at[label_cluster].add(users_wide)
    cluster_grad = prob_sums - label_sums
    leaf_grad = leaf_parts.reshape(OWNERS * TOUCH, LEAVES, E).astype(jnp.bfloat16)
    return user_grad, cluster_grad, leaf_grad
```

```python
import jax
import jax.numpy as jnp
from jax import lax
from jax.experimental import pallas as pl
from jax.experimental.pallas import tpu as pltpu
from jax.sharding import Mesh
from jax.sharding import PartitionSpec as P

BF = jnp.bfloat16
F32 = jnp.float32
LOG2E = 1.4426950408889634
ALL = ("y", "x", "z", "c")
PLANE = ("x", "z")
NT = (((1,), (1,)), ((), ()))
TN = (((0,), (0,)), ((), ()))
META = 128
VMEM = 56 << 20


def params():
    return pltpu.CompilerParams(vmem_limit_bytes=VMEM)


def whole(shape):
    return pl.BlockSpec(shape, lambda *ids: (0,) * len(shape))


def slot_pick(owner_row, slots):
    users = owner_row.shape[1]
    rows = lax.broadcasted_iota(jnp.int32, (users, users), 0)
    cols = lax.broadcasted_iota(jnp.int32, (users, users), 1)
    across = jnp.broadcast_to(owner_row, (users, users))
    down = jnp.sum(jnp.where(rows == cols, across, 0), axis=1, keepdims=True)
    earlier = (across == down) & (rows < cols)
    rank = jnp.sum(earlier.astype(jnp.int32), axis=0, keepdims=True)
    position = owner_row * 2 + rank
    return lax.broadcasted_iota(jnp.int32, (slots, users), 0) == position


def pack_kernel(user_ref, owner_ref, slot_ref, leaf_ref, out_ref):
    slots, width = out_ref.shape[0], user_ref.shape[1]
    users = user_ref.shape[0]
    pick = slot_pick(owner_ref[...], slots).astype(F32).astype(BF)
    out_ref[:, :width] = jnp.dot(pick, user_ref[...], preferred_element_type=F32).astype(BF)
    line = lax.broadcasted_iota(jnp.int32, (META, users), 0)
    leaf = leaf_ref[...]
    meta = jnp.where(line == 0, slot_ref[...] + 1, 0)
    meta = jnp.where(line == 1, leaf >> 6, meta)
    meta = jnp.where(line == 2, leaf & 63, meta)
    meta = meta.astype(F32).astype(BF)
    out_ref[:, width:] = lax.dot_general(pick, meta, NT, preferred_element_type=F32).astype(BF)


def pack(user_vec, owner, slot, leaf, slots):
    users, width = user_vec.shape
    return pl.pallas_call(
        pack_kernel,
        out_shape=jax.ShapeDtypeStruct((slots, width + META), BF),
        name="pack",
    )(user_vec, owner[None], slot[None], leaf[None])


def leaf_kernel(touched_ref, recv_ref, table_ref, cluster_ref, part_ref, grad_ref, label_ref, score_ref):
    k = pl.program_id(0)
    slots, width = part_ref.shape
    leaves = table_ref.shape[1]
    step = 512
    users = recv_ref[:, :width]
    meta = recv_ref[:, width:].astype(F32).T
    slot = meta[0:1, :] - 1.0
    leaf = (meta[1:2, :] * 64.0 + meta[2:3, :]).astype(jnp.int32)
    chosen = slot == k.astype(F32)
    leaf = jnp.where(chosen, leaf, -1)

    @pl.when(k == 0)
    def _():
        line = lax.broadcasted_iota(jnp.int32, (16, slots), 0)
        mine = (jnp.broadcast_to(slot, (16, slots)) == line.astype(F32)).astype(F32).astype(BF)
        label_ref[...] = jnp.dot(mine, users, preferred_element_type=F32)
        clusters = cluster_ref.shape[0]
        line = lax.broadcasted_iota(jnp.int32, (16, clusters), 0)
        column = lax.broadcasted_iota(jnp.int32, (16, clusters), 1)
        target = jnp.where(line == 0, touched_ref[0], jnp.where(line == 1, touched_ref[1], -1))
        pick = (column == target).astype(F32).astype(BF)
        rows = jnp.dot(pick, cluster_ref[...], preferred_element_type=F32).astype(BF)
        part_ref[...] = -lax.dot_general(mine, rows, TN, preferred_element_type=F32)

    peak = None
    for j in range(leaves // step):
        score = lax.dot_general(
            table_ref[0, pl.ds(j * step, step), :], users, NT, preferred_element_type=F32
        )
        score_ref[pl.ds(j * step, step), :] = score
        high = jnp.max(score.reshape(step // 8, 8, slots), axis=0)
        peak = high if peak is None else jnp.maximum(peak, high)
    peak = jnp.max(peak, axis=0, keepdims=True) * LOG2E
    total = jnp.zeros((8, slots), F32)
    for j in range(leaves // step):
        weight = jnp.exp2(score_ref[pl.ds(j * step, step), :] * LOG2E - peak)
        score_ref[pl.ds(j * step, step), :] = weight
        total = total + jnp.sum(weight.reshape(step // 8, 8, slots), axis=0)
    scale = chosen.astype(F32) / jnp.sum(total, axis=0, keepdims=True)
    part = jnp.zeros((slots, width), F32)
    for j in range(leaves // step):
        ids = lax.broadcasted_iota(jnp.int32, (step, slots), 0) + j * step
        coef = score_ref[pl.ds(j * step, step), :] * scale - (ids == leaf).astype(F32)
        coef = coef.astype(BF)
        grad_ref[0, pl.ds(j * step, step), :] = jnp.dot(
            coef, users, preferred_element_type=F32
        ).astype(BF)
        part = part + lax.dot_general(
            coef, table_ref[0, pl.ds(j * step, step), :], TN, preferred_element_type=F32
        )
    part_ref[...] += part


def leaf_pass(touched, recv, leaf_rows, cluster_rows):
    tables, leaves, width = leaf_rows.shape
    slots = recv.shape[0]
    return pl.pallas_call(
        leaf_kernel,
        grid=(tables,),
        in_specs=[
            pl.BlockSpec(memory_space=pltpu.SMEM),
            whole(recv.shape),
            pl.BlockSpec((1, leaves, width), lambda k: (k, 0, 0)),
            whole(cluster_rows.shape),
        ],
        out_specs=[
            whole((slots, width)),
            pl.BlockSpec((1, leaves, width), lambda k: (k, 0, 0)),
            whole((16, width)),
        ],
        out_shape=[
            jax.ShapeDtypeStruct((slots, width), F32),
            jax.ShapeDtypeStruct(leaf_rows.shape, BF),
            jax.ShapeDtypeStruct((16, width), F32),
        ],
        scratch_shapes=[pltpu.VMEM((leaves, slots), F32)],
        compiler_params=params(),
        name="leaf",
    )(touched, recv, leaf_rows, cluster_rows)


def score_kernel(*refs):
    parts = refs[:8]
    user_ref, exp_ref, acc_ref, stat_ref, score_ref, flip_ref = refs[8:]
    step = parts[0].shape[0]
    block, width = user_ref.shape

    @pl.when(pl.program_id(0) == 0)
    def _():
        for j, part in enumerate(parts):
            flip_ref[:, pl.ds(j * step, step)] = part[...].T

    users = user_ref[...]
    peak = None
    for j, part in enumerate(parts):
        score = lax.dot_general(part[...], users, NT, preferred_element_type=F32)
        score_ref[pl.ds(j * step, step), :] = score
        high = jnp.max(score.reshape(step // 8, 8, block), axis=0)
        peak = high if peak is None else jnp.maximum(peak, high)
    peak = jnp.max(peak, axis=0, keepdims=True)
    scaled = peak * LOG2E
    total = jnp.zeros((8, block), F32)
    acc = jnp.zeros((width, block), F32)
    for j in range(len(parts)):
        weight = jnp.exp2(score_ref[pl.ds(j * step, step), :] * LOG2E - scaled)
        total = total + jnp.sum(weight.reshape(step // 8, 8, block), axis=0)
        weight = weight.astype(BF)
        exp_ref[pl.ds(j * step, step), :] = weight
        acc = acc + jnp.dot(
            flip_ref[:, pl.ds(j * step, step)], weight, preferred_element_type=F32
        )
    acc_ref[...] = acc.T.astype(BF)
    stat_ref[0:1, :] = peak
    stat_ref[1:2, :] = jnp.sum(total, axis=0, keepdims=True)


def score_pass(parts, users):
    step, width = parts[0].shape
    clusters = step * len(parts)
    count = users.shape[0]
    block = 512
    return pl.pallas_call(
        score_kernel,
        grid=(count // block,),
        in_specs=[whole((step, width))] * len(parts)
        + [pl.BlockSpec((block, width), lambda i: (i, 0))],
        out_specs=[
            pl.BlockSpec((clusters, block), lambda i: (0, i)),
            pl.BlockSpec((block, width), lambda i: (i, 0)),
            pl.BlockSpec((2, block), lambda i: (0, i)),
        ],
        out_shape=[
            jax.ShapeDtypeStruct((clusters, count), BF),
            jax.ShapeDtypeStruct((count, width), BF),
            jax.ShapeDtypeStruct((2, count), F32),
        ],
        scratch_shapes=[
            pltpu.VMEM((clusters, block), F32),
            pltpu.VMEM((width, clusters), BF),
        ],
        compiler_params=params(),
        name="scores",
    )(*parts, users)


def merge_stats(stats):
    peak = jnp.max(stats[:, 0, :], axis=0, keepdims=True)
    total = jnp.sum(stats[:, 1, :] * jnp.exp(stats[:, 0, :] - peak), axis=0, keepdims=True)
    return peak, total


def scale_kernel(stats_ref, mine_ref, user_ref, out_ref):
    peak, total = merge_stats(stats_ref[...])
    weight = jnp.exp(mine_ref[0:1, :] - peak) / total
    weight = jnp.broadcast_to(weight, (128, weight.shape[1])).T
    out_ref[...] = (user_ref[...].astype(F32) * weight[:, 0:1]).astype(BF)


def scale_users(stats, mine, users):
    return pl.pallas_call(
        scale_kernel,
        out_shape=jax.ShapeDtypeStruct(users.shape, BF),
        compiler_params=params(),
        name="scale_users",
    )(stats, mine, users)


def cluster_kernel(exp_ref, user_ref, out_ref):
    out_ref[...] = jnp.dot(exp_ref[...], user_ref[...], preferred_element_type=F32)


def cluster_pass(weights, users, half):
    clusters, count = weights.shape
    width = users.shape[1]
    block = 1024
    steps = clusters // 2 // block
    return pl.pallas_call(
        cluster_kernel,
        grid=(steps,),
        in_specs=[
            pl.BlockSpec((block, count), lambda i: (i + half * steps, 0)),
            whole((count, width)),
        ],
        out_specs=pl.BlockSpec((block, width), lambda i: (i, 0)),
        out_shape=jax.ShapeDtypeStruct((clusters // 2, width), F32),
        compiler_params=params(),
        name="cluster_sums",
    )(weights, users)


def home_kernel(acc_ref, stats_ref, owner_ref, back_ref, out_ref):
    peers, users, width = acc_ref.shape
    stats = stats_ref[...]
    peak, total = merge_stats(stats)
    factor = jnp.exp(stats[:, 0, :] - peak) / total
    factor = factor.T
    slots = back_ref.shape[0]
    pick = slot_pick(owner_ref[...], slots).astype(F32)
    out = lax.dot_general(
        pick, back_ref[...], TN, preferred_element_type=F32, precision=lax.Precision.HIGHEST
    )
    for q in range(peers):
        out = out + acc_ref[q].astype(F32) * factor[:, q : q + 1]
    out_ref[...] = out


def home_pass(acc, stats, owner, back):
    return pl.pallas_call(
        home_kernel,
        out_shape=jax.ShapeDtypeStruct(acc.shape[1:], F32),
        compiler_params=params(),
        name="home",
    )(acc, stats, owner[None], back)


def shift(x, axis, by):
    size = lax.axis_size(axis)
    return lax.ppermute(x, axis, [(i, (i + by) % size) for i in range(size)])


def swap(x, axis):
    return lax.all_to_all(x, axis, 0, 0, tiled=True)


def per_device(user_vec, cluster_rows, leaf_rows, touched, route_owner, route_slot, leaf_label):
    owners = lax.axis_size(ALL)
    rows = lax.axis_size("y")
    peers = lax.axis_size(PLANE)
    count, width = user_vec.shape
    slots = 2 * owners

    users = swap(jnp.broadcast_to(user_vec[None], (peers, count, width)), PLANE)
    users = users.reshape(peers * count, width)
    near = [cluster_rows] + [shift(cluster_rows, "y", -j) for j in range(1, rows)]
    far = [shift(part, "c", 1) for part in near]

    sent = pack(user_vec, route_owner, route_slot, leaf_label, slots)
    recv = swap(sent.reshape(owners, 2, width + META), ALL).reshape(slots, width + META)

    weights, acc, mine = score_pass(near + far, users)
    stats = swap(jnp.broadcast_to(mine[None], (peers,) + mine.shape), PLANE)
    acc = swap(acc.reshape(peers, count, width), PLANE)

    leaf_part, leaf_grad, labels = leaf_pass(touched, recv, leaf_rows, cluster_rows)
    back = swap(leaf_part.reshape(owners, 2, width), ALL).reshape(slots, width)

    scaled = scale_users(stats, mine, users)
    other = shift(cluster_pass(weights, scaled, 1), "c", 1)
    both = (cluster_pass(weights, scaled, 0) + other).reshape(rows, -1, width)
    cluster_grad = both[0]
    for j in range(1, rows):
        cluster_grad = cluster_grad + shift(both[j].astype(BF), "y", j).astype(F32)
    ids = jnp.arange(cluster_rows.shape[0])[:, None]
    for k in range(2):
        cluster_grad = cluster_grad - jnp.where(ids == touched[k], labels[k][None], 0.0)

    place = lax.axis_index(PLANE)
    stats_home = lax.dynamic_slice_in_dim(stats, place * count, count, 2)
    user_grad = home_pass(acc, stats_home, route_owner, back)
    return user_grad, cluster_grad, leaf_grad


def solution(mesh):
    grid = Mesh(mesh.devices.reshape(4, 4, 4, 2), ALL)
    one = P(ALL)
    return jax.shard_map(
        per_device,
        mesh=grid,
        in_specs=(P(ALL, None), P(ALL, None), P(ALL, None, None), one, one, one, one),
        out_specs=(P(ALL, None), P(ALL, None), P(ALL, None, None)),
        check_vma=False,
    )
```

```python
import jax
import jax.numpy as jnp
from jax import lax
from jax.experimental import pallas as pl
from jax.experimental.pallas import tpu as pltpu
from jax.sharding import Mesh
from jax.sharding import PartitionSpec as P

BF = jnp.bfloat16
F32 = jnp.float32
LOG2E = 1.4426950408889634
ALL = ("y", "x", "z", "c")
PLANE = ("x", "z")
NT = (((1,), (1,)), ((), ()))
TN = (((0,), (0,)), ((), ()))
META = 128
EXTRA = 16
LANES = 128


def params(mib):
    return pltpu.CompilerParams(vmem_limit_bytes=mib << 20)


def cost(flops, transcendentals, moved):
    return pl.CostEstimate(
        flops=flops, transcendentals=transcendentals, bytes_accessed=moved
    )


def whole(shape):
    return pl.BlockSpec(shape, lambda *ids: (0,) * len(shape))


def prep_kernel(user_ref, owner_ref, slot_ref, leaf_ref, out_ref):
    count, width = user_ref.shape
    out_ref[:count, :] = user_ref[...]
    line = lax.broadcasted_iota(jnp.int32, (EXTRA, count), 0)
    leaf = leaf_ref[...]
    left = jnp.where(line == 0, owner_ref[...], jnp.where(line == 1, leaf >> 6, 0))
    right = jnp.where(line == 0, slot_ref[...] + 1, jnp.where(line == 1, leaf & 63, 0))
    both = jnp.concatenate([left, right], axis=1)
    out_ref[count:, :] = both.astype(F32).astype(BF)


def prep(user_vec, owner, slot, leaf):
    count, width = user_vec.shape
    return pl.pallas_call(
        prep_kernel,
        out_shape=jax.ShapeDtypeStruct((count + EXTRA, width), BF),
        name="prep",
    )(user_vec, owner[None], slot[None], leaf[None])


def select_kernel(place_ref, *refs):
    chunks = refs[:4]
    users_ref, pick_ref = refs[4:6]
    sends = refs[6:10]
    owner_ref, slot_ref, high_ref, low_ref, rows_ref = refs[10:]
    count = LANES
    height = count + EXTRA
    width = users_ref.shape[1]
    homes = users_ref.shape[0] // count
    y, x, z, c = (place_ref[i] for i in range(4))
    for k, chunk in enumerate(chunks):
        for j in range(4):
            home = ((x + j) & 3) * 4 + ((z + k) & 3)
            users_ref[pl.ds(pl.multiple_of(home * count, count), count), :] = chunk[
                pl.ds(j * height, count), :
            ]
            extra = chunk[pl.ds(j * height + count, EXTRA), :].astype(F32)
            at = pl.ds(home, 1)
            owner_ref[at, :] = extra[0:1, :count]
            slot_ref[at, :] = extra[0:1, count:]
            high_ref[at, :] = extra[1:2, :count]
            low_ref[at, :] = extra[1:2, count:]

    line = lax.broadcasted_iota(jnp.int32, (8, count), 0)
    target = ((y + (line & 3)) & 3) * 32 + x * 8 + z * 2 + (c ^ (line >> 2))
    target = target.astype(F32)
    match = jnp.concatenate(
        [
            (jnp.broadcast_to(owner_ref[h : h + 1, :], (8, count)) == target).astype(F32)
            for h in range(homes)
        ],
        axis=0,
    )
    rows = lax.broadcasted_iota(jnp.int32, (count, count), 0)
    cols = lax.broadcasted_iota(jnp.int32, (count, count), 1)
    before = (rows < cols).astype(F32).astype(BF)
    rank = jnp.dot(match.astype(BF), before, preferred_element_type=F32)
    first = match * (rank == 0.0).astype(F32)
    second = match * (rank == 1.0).astype(F32)
    lines = lax.broadcasted_iota(jnp.int32, (LANES, count), 0)
    for h in range(homes):
        part = slice(h * 8, (h + 1) * 8)
        pick = jnp.concatenate([first[part], second[part]], axis=0).astype(BF)
        pick_ref[pl.ds(h * 16, 16), :] = pick
        rows_ref[h, :, :width] = jnp.dot(
            pick, users_ref[pl.ds(h * count, count), :], preferred_element_type=F32
        )
        meta = jnp.where(lines == 0, slot_ref[h : h + 1, :], 0.0)
        meta = jnp.where(lines == 1, high_ref[h : h + 1, :], meta)
        meta = jnp.where(lines == 2, low_ref[h : h + 1, :], meta)
        rows_ref[h, :, width:] = lax.dot_general(
            pick, meta.astype(BF), NT, preferred_element_type=F32
        )
    for dy, send in enumerate(sends):
        for core in range(2):
            for r in range(2):
                send[pl.ds(core * 32 + r * 16, 16), :] = rows_ref[
                    :, r * 8 + core * 4 + dy, :
                ].astype(BF)


def select_pass(place, chunks):
    width = chunks[0].shape[1]
    homes = 4 * len(chunks)
    users = homes * LANES
    return pl.pallas_call(
        select_kernel,
        in_specs=[pl.BlockSpec(memory_space=pltpu.SMEM)]
        + [pl.BlockSpec(memory_space=pltpu.VMEM)] * 4,
        out_shape=[
            jax.ShapeDtypeStruct((users, width), BF),
            jax.ShapeDtypeStruct((homes * 16, LANES), BF),
        ]
        + [jax.ShapeDtypeStruct((64, width + META), BF)] * 4,
        scratch_shapes=[pltpu.VMEM((homes, LANES), F32)] * 4
        + [pltpu.VMEM((homes, 16, width + META), F32)],
        compiler_params=params(16),
        name="select",
    )(place, *chunks)


def leaf_kernel(*refs):
    touched_ref, own, other = refs[0], refs[1:5], refs[5:9]
    table_ref, cluster_ref = refs[9:11]
    backs, (grad_ref, label_ref, score_ref, recv_ref, part_ref) = refs[12:16], refs[16:]
    k = pl.program_id(0)
    slots, width = part_ref.shape

    @pl.when(k == 0)
    def _():
        for dy in range(4):
            recv_ref[pl.ds(dy * 64, 32), :] = own[dy][pl.ds(0, 32), :]
            recv_ref[pl.ds(dy * 64 + 32, 32), :] = other[dy][pl.ds(32, 32), :]

    leaves = table_ref.shape[1]
    step = 512
    users = recv_ref[:, :width]
    meta = recv_ref[:, width:].astype(F32).T
    slot = meta[0:1, :] - 1.0
    leaf = (meta[1:2, :] * 64.0 + meta[2:3, :]).astype(jnp.int32)
    chosen = slot == k.astype(F32)
    leaf = jnp.where(chosen, leaf, -1)

    @pl.when(k == 0)
    def _():
        line = lax.broadcasted_iota(jnp.int32, (16, slots), 0)
        mine = (jnp.broadcast_to(slot, (16, slots)) == line.astype(F32)).astype(F32).astype(BF)
        label_ref[...] = jnp.dot(mine, users, preferred_element_type=F32)
        clusters = cluster_ref.shape[0]
        line = lax.broadcasted_iota(jnp.int32, (16, clusters), 0)
        column = lax.broadcasted_iota(jnp.int32, (16, clusters), 1)
        target = jnp.where(line == 0, touched_ref[0], jnp.where(line == 1, touched_ref[1], -1))
        pick = (column == target).astype(F32).astype(BF)
        rows = jnp.dot(pick, cluster_ref[...], preferred_element_type=F32).astype(BF)
        part_ref[...] = -lax.dot_general(mine, rows, TN, preferred_element_type=F32)

    peak = None
    for j in range(leaves // step):
        score = lax.dot_general(
            table_ref[0, pl.ds(j * step, step), :], users, NT, preferred_element_type=F32
        )
        score_ref[pl.ds(j * step, step), :] = score
        high = jnp.max(score.reshape(step // 8, 8, slots), axis=0)
        peak = high if peak is None else jnp.maximum(peak, high)
    peak = jnp.max(peak, axis=0, keepdims=True) * LOG2E
    total = jnp.zeros((8, slots), F32)
    for j in range(leaves // step):
        weight = jnp.exp2(score_ref[pl.ds(j * step, step), :] * LOG2E - peak)
        score_ref[pl.ds(j * step, step), :] = weight
        total = total + jnp.sum(weight.reshape(step // 8, 8, slots), axis=0)
    scale = chosen.astype(F32) / jnp.sum(total, axis=0, keepdims=True)
    part = jnp.zeros((slots, width), F32)
    for j in range(leaves // step):
        ids = lax.broadcasted_iota(jnp.int32, (step, slots), 0) + j * step
        coef = score_ref[pl.ds(j * step, step), :] * scale - (ids == leaf).astype(F32)
        coef = coef.astype(BF)
        grad_ref[0, pl.ds(j * step, step), :] = jnp.dot(
            coef, users, preferred_element_type=F32
        ).astype(BF)
        part = part + lax.dot_general(
            coef, table_ref[0, pl.ds(j * step, step), :], TN, preferred_element_type=F32
        )
    part_ref[...] += part

    @pl.when(k == pl.num_programs(0) - 1)
    def _():
        for dy, back in enumerate(backs):
            back[...] = part_ref[pl.ds(dy * 64, 64), :]


def leaf_pass(touched, own, other, leaf_rows, cluster_rows, after):
    tables, leaves, width = leaf_rows.shape
    slots = 4 * own[0].shape[0]
    return pl.pallas_call(
        leaf_kernel,
        grid=(tables,),
        in_specs=[pl.BlockSpec(memory_space=pltpu.SMEM)]
        + [whole(own[0].shape)] * 8
        + [
            pl.BlockSpec((1, leaves, width), lambda k: (k, 0, 0)),
            whole(cluster_rows.shape),
            pl.BlockSpec(memory_space=pl.ANY),
        ],
        out_specs=[whole((64, width))] * 4
        + [
            pl.BlockSpec((1, leaves, width), lambda k: (k, 0, 0)),
            whole((16, width)),
        ],
        out_shape=[jax.ShapeDtypeStruct((64, width), F32)] * 4
        + [
            jax.ShapeDtypeStruct(leaf_rows.shape, BF),
            jax.ShapeDtypeStruct((16, width), F32),
        ],
        scratch_shapes=[
            pltpu.VMEM((leaves, slots), F32),
            pltpu.VMEM((slots, width + META), BF),
            pltpu.VMEM((slots, width), F32),
        ],
        compiler_params=params(24),
        cost_estimate=cost(6 * tables * leaves * slots * width, tables * leaves * slots, 8 << 20),
        name="leaf",
    )(touched, *own, *other, leaf_rows, cluster_rows, after)


def score_kernel(*refs):
    parts, users_ref = refs[:8], refs[8]
    acc_ref, stat_ref, spread_ref, first_ref, second_ref, flip_ref = refs[10:]
    step, width = parts[0].shape
    tiles = 4
    block = users_ref.shape[0] // tiles
    scores = (first_ref, second_ref)
    for j, part in enumerate(parts):
        flip_ref[:, pl.ds(j * step, step)] = part[...].T

    def score(tile, j, peak):
        out = lax.dot_general(
            parts[j][...],
            users_ref[pl.ds(tile * block, block), :],
            NT,
            preferred_element_type=F32,
        )
        scores[tile % 2][pl.ds(j * step, step), :] = out
        high = jnp.max(out.reshape(step // 8, 8, block), axis=0)
        return high if peak is None else jnp.maximum(peak, high)

    peak = None
    for j in range(len(parts)):
        peak = score(0, j, peak)
    for tile in range(tiles):
        top = jnp.max(peak, axis=0, keepdims=True) * LOG2E
        peak = None
        total = jnp.zeros((8, block), F32)
        acc = jnp.zeros((width, block), F32)
        for j in range(len(parts)):
            if tile + 1 < tiles:
                peak = score(tile + 1, j, peak)
            weight = jnp.exp2(scores[tile % 2][pl.ds(j * step, step), :] * LOG2E - top)
            total = total + jnp.sum(weight.reshape(step // 8, 8, block), axis=0)
            acc = acc + jnp.dot(
                flip_ref[:, pl.ds(j * step, step)], weight.astype(BF), preferred_element_type=F32
            )
        at = pl.ds(tile * block, block)
        acc_ref[at, :] = acc.T.astype(BF)
        stat_ref[0:1, at] = top
        stat_ref[1:2, at] = jnp.sum(total, axis=0, keepdims=True)
    for q in range(spread_ref.shape[0]):
        spread_ref[q] = stat_ref[...]


def score_pass(parts, users, *after):
    step, width = parts[0].shape
    clusters, count = step * len(parts), users.shape[0]
    peers = count // LANES
    return pl.pallas_call(
        score_kernel,
        in_specs=[pl.BlockSpec(memory_space=pltpu.VMEM)] * 9
        + [pl.BlockSpec(memory_space=pl.ANY)] * len(after),
        out_shape=[
            jax.ShapeDtypeStruct((count, width), BF),
            jax.ShapeDtypeStruct((2, count), F32),
            jax.ShapeDtypeStruct((peers, 2, count), F32),
        ],
        scratch_shapes=[
            pltpu.VMEM((clusters, count // 4), F32),
            pltpu.VMEM((clusters, count // 4), F32),
            pltpu.VMEM((width, clusters), BF),
        ],
        compiler_params=params(36),
        cost_estimate=cost(4 * count * clusters * width, count * clusters, 6 << 20),
        name="scores",
    )(*parts, users, *after)


def merge_stats(stats):
    peak = jnp.max(stats[:, 0, :], axis=0, keepdims=True)
    total = jnp.sum(stats[:, 1, :] * jnp.exp2(stats[:, 0, :] - peak), axis=0, keepdims=True)
    return peak, total


def cluster_tiles(parts, users_ref, log_row, out_refs, scores, others):
    def score(j):
        scores[j % 2][...] = lax.dot_general(
            parts[j][...], users_ref[...], NT, preferred_element_type=F32
        )

    score(0)
    for j, out_ref in enumerate(out_refs):
        if j + 1 < len(parts):
            score(j + 1)
        prob = jnp.exp2(scores[j % 2][...] * LOG2E - log_row).astype(BF)
        out = jnp.dot(prob, users_ref[...], preferred_element_type=F32)
        if others:
            out = out + others[j][...]
        out_ref[...] = out.astype(out_ref.dtype)


def first_cluster_kernel(count, *refs):
    stats_ref, users_ref = refs[:2]
    parts = refs[2 : 2 + count]
    outs = refs[3 + count : 3 + 2 * count]
    log_ref = refs[3 + 2 * count]
    peak, total = merge_stats(stats_ref[...])
    log_row = peak + jnp.log2(total)
    log_ref[...] = log_row
    cluster_tiles(parts, users_ref, log_row, outs, refs[-2:], ())


def later_cluster_kernel(count, added, *refs):
    log_ref, users_ref = refs[:2]
    parts = refs[2 : 2 + count]
    others = refs[2 + count : 2 + count + added]
    outs = refs[3 + count + added : 3 + 2 * count + added]
    cluster_tiles(parts, users_ref, log_ref[...], outs, refs[-2:], others)


def cluster_pass(stats, users, parts, others, dtype, after, first):
    count, width = users.shape
    block = parts[0].shape[0]
    outs = [jax.ShapeDtypeStruct((block, width), dtype)] * len(parts)
    if first:
        outs.append(jax.ShapeDtypeStruct((1, count), F32))
        kernel = lambda *refs: first_cluster_kernel(len(parts), *refs)
    else:
        kernel = lambda *refs: later_cluster_kernel(len(parts), len(others), *refs)
    return pl.pallas_call(
        kernel,
        in_specs=[pl.BlockSpec(memory_space=pltpu.VMEM)] * (2 + len(parts) + len(others))
        + [pl.BlockSpec(memory_space=pl.ANY)],
        out_shape=outs,
        scratch_shapes=[pltpu.VMEM((block, count), F32)] * 2,
        compiler_params=params(24),
        cost_estimate=cost(
            4 * block * len(parts) * count * width, block * len(parts) * count, 3 << 20
        ),
        name="cluster_sums",
    )(stats, users, *parts, *others, after)


def fold_kernel(*refs):
    acc_ref, stat_ref, log_ref, pick_ref = refs[:4]
    own, other = refs[4:8], refs[8:12]
    out_ref, rows_ref = refs[12:]
    homes = out_ref.shape[0]
    for core, sides in enumerate((own, other)):
        for dy, side in enumerate(sides):
            for r in range(2):
                rows_ref[r * 8 + core * 4 + dy] = side[pl.ds(core * 32 + r * 16, 16), :]
    factor = jnp.exp2(stat_ref[0:1, :] - log_ref[...])
    factor = jnp.concatenate(
        [factor[:, h * LANES : (h + 1) * LANES] for h in range(homes)], axis=0
    ).T
    for h in range(homes):
        pick = pick_ref[pl.ds(h * 16, 16), :].astype(F32)
        leaf = lax.dot_general(
            pick, rows_ref[:, h, :], TN, preferred_element_type=F32, precision=lax.Precision.HIGHEST
        )
        acc = acc_ref[pl.ds(h * LANES, LANES), :].astype(F32) * factor[:, h : h + 1]
        out_ref[h] = (acc + leaf).astype(BF)


def fold_pass(acc, mine, log_row, picks, own, other):
    count, width = acc.shape
    homes = count // LANES
    return pl.pallas_call(
        fold_kernel,
        out_shape=jax.ShapeDtypeStruct((homes, LANES, width), BF),
        scratch_shapes=[pltpu.VMEM((16, homes, width), F32)],
        compiler_params=params(16),
        name="fold",
    )(acc, mine, log_row, picks, *own, *other)


def home_kernel(acc_ref, out_ref):
    out = acc_ref[0].astype(F32)
    for q in range(1, acc_ref.shape[0]):
        out = out + acc_ref[q].astype(F32)
    out_ref[...] = out


def home_pass(acc):
    return pl.pallas_call(
        home_kernel,
        out_shape=jax.ShapeDtypeStruct(acc.shape[1:], F32),
        compiler_params=params(16),
        name="home",
    )(acc)


def last_kernel(touched_ref, own_ref, a_ref, b_ref, c_ref, label_ref, out_ref):
    out = own_ref[...]
    for ref in (a_ref, b_ref, c_ref):
        out = out + ref[...].astype(F32)
    ids = lax.broadcasted_iota(jnp.int32, out.shape, 0)
    for k in range(2):
        out = out - jnp.where(ids == touched_ref[k], label_ref[k : k + 1, :], 0.0)
    out_ref[...] = out


def last_pass(touched, own, others, labels):
    return pl.pallas_call(
        last_kernel,
        in_specs=[pl.BlockSpec(memory_space=pltpu.SMEM)]
        + [pl.BlockSpec(memory_space=pltpu.VMEM)] * 5,
        out_shape=jax.ShapeDtypeStruct(own.shape, F32),
        compiler_params=params(16),
        name="cluster_home",
    )(touched, own, *others, labels)


def shift(x, axis, by):
    size = lax.axis_size(axis)
    return lax.ppermute(x, axis, [(i, (i + by) % size) for i in range(size)])


def swap(x, axis):
    return lax.all_to_all(x, axis, 0, 0, tiled=True)


def per_device(user_vec, cluster_rows, leaf_rows, touched, route_owner, route_slot, leaf_label):
    hops = range(1, 4)
    place = jnp.stack([lax.axis_index(name) for name in ALL]).astype(jnp.int32)

    ready = prep(user_vec, route_owner, route_slot, leaf_label)
    line = jnp.concatenate([ready] + [shift(ready, "x", -j) for j in hops], axis=0)
    near = [cluster_rows] + [shift(cluster_rows, "y", -j) for j in hops]
    chunks = [line] + [shift(line, "z", -k) for k in hops]
    far = [shift(part, "c", 1) for part in near]

    users, picks, *sends = select_pass(place, chunks)
    came = [sends[0]] + [shift(sends[j], "y", j) for j in hops]
    acc, mine, spread = score_pass(near + far, users, sends[0])
    stats = swap(spread, PLANE)
    cross = [shift(x, "c", 1) for x in came]

    *back, leaf_grad, labels = leaf_pass(touched, came, cross, leaf_rows, cluster_rows, mine)
    back = [back[0]] + [shift(back[j], "y", -j) for j in hops]

    *away, log_row = cluster_pass(stats, users, far[1:], (), F32, labels, True)
    away = [shift(x, "c", 1) for x in away]
    (away_own,) = cluster_pass(log_row, users, far[:1], (), F32, log_row, False)
    away_own = shift(away_own, "c", 1)
    cross = [shift(x, "c", 1) for x in back]
    acc = swap(fold_pass(acc, mine, log_row, picks, back, cross), PLANE)
    both = cluster_pass(log_row, users, near[1:], away, BF, away_own, False)
    arrived = [shift(x, "y", j) for j, x in zip(hops, both)]
    (own,) = cluster_pass(log_row, users, near[:1], [away_own], F32, both[0], False)
    cluster_grad = last_pass(touched, own, arrived, labels)
    user_grad = home_pass(acc)
    return user_grad, cluster_grad, leaf_grad


def solution(mesh):
    grid = Mesh(mesh.devices.reshape(4, 4, 4, 2), ALL)
    one = P(ALL)
    return jax.shard_map(
        per_device,
        mesh=grid,
        in_specs=(P(ALL, None), P(ALL, None), P(ALL, None, None), one, one, one, one),
        out_specs=(P(ALL, None), P(ALL, None), P(ALL, None, None)),
        check_vma=False,
    )
```

```python
import jax
import jax.numpy as jnp
from jax import lax
from jax.experimental import pallas as pl
from jax.experimental.pallas import tpu as pltpu
from jax.sharding import Mesh
from jax.sharding import PartitionSpec as P

BF = jnp.bfloat16
F32 = jnp.float32
LOG2E = 1.4426950408889634
ALL = ("y", "x", "z", "c")
PLANE = ("x", "z")
NT = (((1,), (1,)), ((), ()))
TN = (((0,), (0,)), ((), ()))
META = 128
EXTRA = 16
LANES = 128


def params(mib):
    return pltpu.CompilerParams(vmem_limit_bytes=mib << 20)


def cost(flops, transcendentals, moved):
    return pl.CostEstimate(
        flops=flops, transcendentals=transcendentals, bytes_accessed=moved
    )


def whole(shape):
    return pl.BlockSpec(shape, lambda *ids: (0,) * len(shape))


def prep_kernel(user_ref, owner_ref, slot_ref, leaf_ref, out_ref):
    count, width = user_ref.shape
    for j in range(out_ref.shape[0]):
        out_ref[j, :count, :] = user_ref[...]
    line = lax.broadcasted_iota(jnp.int32, (EXTRA, count), 0)
    leaf = leaf_ref[...]
    left = jnp.where(line == 0, owner_ref[...], jnp.where(line == 1, leaf >> 6, 0))
    right = jnp.where(line == 0, slot_ref[...] + 1, jnp.where(line == 1, leaf & 63, 0))
    both = jnp.concatenate([left, right], axis=1)
    for j in range(out_ref.shape[0]):
        out_ref[j, count:, :] = both.astype(F32).astype(BF)


def prep(user_vec, owner, slot, leaf):
    count, width = user_vec.shape
    return pl.pallas_call(
        prep_kernel,
        out_shape=jax.ShapeDtypeStruct((16, count + EXTRA, width), BF),
        name="prep",
    )(user_vec, owner[None], slot[None], leaf[None])


def select_kernel(place_ref, plane_ref, *refs):
    users_ref, pick_ref = refs[:2]
    sends = refs[2:6]
    owner_ref, slot_ref, high_ref, low_ref, rows_ref = refs[6:]
    count = LANES
    width = users_ref.shape[1]
    homes = users_ref.shape[0] // count
    y, x, z, c = (place_ref[i] for i in range(4))
    for home in range(homes):
        users_ref[pl.ds(home * count, count), :] = plane_ref[home, :count, :]
        extra = plane_ref[home, count:, :].astype(F32)
        at = pl.ds(home, 1)
        owner_ref[at, :] = extra[0:1, :count]
        slot_ref[at, :] = extra[0:1, count:]
        high_ref[at, :] = extra[1:2, :count]
        low_ref[at, :] = extra[1:2, count:]

    line = lax.broadcasted_iota(jnp.int32, (8, count), 0)
    target = ((y + (line & 3)) & 3) * 32 + x * 8 + z * 2 + (c ^ (line >> 2))
    target = target.astype(F32)
    match = jnp.concatenate(
        [
            (jnp.broadcast_to(owner_ref[h : h + 1, :], (8, count)) == target).astype(F32)
            for h in range(homes)
        ],
        axis=0,
    )
    rows = lax.broadcasted_iota(jnp.int32, (count, count), 0)
    cols = lax.broadcasted_iota(jnp.int32, (count, count), 1)
    before = (rows < cols).astype(F32).astype(BF)
    rank = jnp.dot(match.astype(BF), before, preferred_element_type=F32)
    first = match * (rank == 0.0).astype(F32)
    second = match * (rank == 1.0).astype(F32)
    lines = lax.broadcasted_iota(jnp.int32, (LANES, count), 0)
    for h in range(homes):
        part = slice(h * 8, (h + 1) * 8)
        pick = jnp.concatenate([first[part], second[part]], axis=0).astype(BF)
        pick_ref[pl.ds(h * 16, 16), :] = pick
        rows_ref[h, :, :width] = jnp.dot(
            pick, users_ref[pl.ds(h * count, count), :], preferred_element_type=F32
        )
        meta = jnp.where(lines == 0, slot_ref[h : h + 1, :], 0.0)
        meta = jnp.where(lines == 1, high_ref[h : h + 1, :], meta)
        meta = jnp.where(lines == 2, low_ref[h : h + 1, :], meta)
        rows_ref[h, :, width:] = lax.dot_general(
            pick, meta.astype(BF), NT, preferred_element_type=F32
        )
    for dy, send in enumerate(sends):
        for core in range(2):
            for r in range(2):
                send[pl.ds(core * 32 + r * 16, 16), :] = rows_ref[
                    :, r * 8 + core * 4 + dy, :
                ].astype(BF)


def select_pass(place, plane):
    homes, _, width = plane.shape
    users = homes * LANES
    return pl.pallas_call(
        select_kernel,
        in_specs=[pl.BlockSpec(memory_space=pltpu.SMEM)]
        + [pl.BlockSpec(memory_space=pltpu.VMEM)],
        out_shape=[
            jax.ShapeDtypeStruct((users, width), BF),
            jax.ShapeDtypeStruct((homes * 16, LANES), BF),
        ]
        + [jax.ShapeDtypeStruct((64, width + META), BF)] * 4,
        scratch_shapes=[pltpu.VMEM((homes, LANES), F32)] * 4
        + [pltpu.VMEM((homes, 16, width + META), F32)],
        compiler_params=params(16),
        name="select",
    )(place, plane)


def leaf_kernel(*refs):
    touched_ref, own_ref, other_ref, stat_ref, table_ref, cluster_ref = refs[:6]
    back_ref, grad_ref, label_ref, score_ref, recv_ref, part_ref = refs[6:]
    k = pl.program_id(0)
    slots, width = part_ref.shape

    @pl.when(k == 0)
    def _():
        for dy in range(4):
            near, far = pl.ds(dy * 64, 32), pl.ds(dy * 64 + 32, 32)
            recv_ref[near, :] = own_ref[near, :]
            recv_ref[far, :] = other_ref[far, :]

    leaves = table_ref.shape[1]
    step = 512
    users = recv_ref[:, :width]
    meta = recv_ref[:, width:].astype(F32).T
    slot = meta[0:1, :] - 1.0
    leaf = (meta[1:2, :] * 64.0 + meta[2:3, :]).astype(jnp.int32)
    chosen = slot == k.astype(F32)
    leaf = jnp.where(chosen, leaf, -1)

    @pl.when(k == 0)
    def _():
        line = lax.broadcasted_iota(jnp.int32, (16, slots), 0)
        mine = (jnp.broadcast_to(slot, (16, slots)) == line.astype(F32)).astype(F32).astype(BF)
        label_ref[...] = jnp.dot(mine, users, preferred_element_type=F32)
        clusters = cluster_ref.shape[0]
        line = lax.broadcasted_iota(jnp.int32, (16, clusters), 0)
        column = lax.broadcasted_iota(jnp.int32, (16, clusters), 1)
        target = jnp.where(line == 0, touched_ref[0], jnp.where(line == 1, touched_ref[1], -1))
        pick = (column == target).astype(F32).astype(BF)
        rows = jnp.dot(pick, cluster_ref[...], preferred_element_type=F32).astype(BF)
        part_ref[...] = -lax.dot_general(mine, rows, TN, preferred_element_type=F32)

    peak = None
    for j in range(leaves // step):
        score = lax.dot_general(
            table_ref[0, pl.ds(j * step, step), :], users, NT, preferred_element_type=F32
        )
        score_ref[pl.ds(j * step, step), :] = score
        high = jnp.max(score.reshape(step // 8, 8, slots), axis=0)
        peak = high if peak is None else jnp.maximum(peak, high)
    peak = jnp.max(peak, axis=0, keepdims=True) * LOG2E
    total = jnp.zeros((8, slots), F32)
    for j in range(leaves // step):
        weight = jnp.exp2(score_ref[pl.ds(j * step, step), :] * LOG2E - peak)
        score_ref[pl.ds(j * step, step), :] = weight
        total = total + jnp.sum(weight.reshape(step // 8, 8, slots), axis=0)
    scale = chosen.astype(F32) / jnp.sum(total, axis=0, keepdims=True)
    part = jnp.zeros((slots, width), F32)
    for j in range(leaves // step):
        ids = lax.broadcasted_iota(jnp.int32, (step, slots), 0) + j * step
        coef = score_ref[pl.ds(j * step, step), :] * scale - (ids == leaf).astype(F32)
        coef = coef.astype(BF)
        grad_ref[0, pl.ds(j * step, step), :] = jnp.dot(
            coef, users, preferred_element_type=F32
        ).astype(BF)
        part = part + lax.dot_general(
            coef, table_ref[0, pl.ds(j * step, step), :], TN, preferred_element_type=F32
        )
    part_ref[...] += part

    @pl.when(k == pl.num_programs(0) - 1)
    def _():
        peers = back_ref.shape[0]
        for j in range(8):
            at = slice(j * width, (j + 1) * width)
            back_ref[:, j, :] = jnp.broadcast_to(stat_ref[0:1, at], (peers, width))
            back_ref[:, 8 + j, :] = jnp.broadcast_to(stat_ref[1:2, at], (peers, width))
        for j in range(16):
            back_ref[:, 16 + j, :] = part_ref[pl.ds(j * peers, peers), :]


def leaf_pass(touched, own, other, stats, leaf_rows, cluster_rows):
    tables, leaves, width = leaf_rows.shape
    slots = own.shape[0]
    peers = slots // 16
    return pl.pallas_call(
        leaf_kernel,
        grid=(tables,),
        in_specs=[
            pl.BlockSpec(memory_space=pltpu.SMEM),
            whole(own.shape),
            whole(other.shape),
            whole(stats.shape),
            pl.BlockSpec((1, leaves, width), lambda k: (k, 0, 0)),
            whole(cluster_rows.shape),
        ],
        out_specs=[
            whole((peers, 32, width)),
            pl.BlockSpec((1, leaves, width), lambda k: (k, 0, 0)),
            whole((16, width)),
        ],
        out_shape=[
            jax.ShapeDtypeStruct((peers, 32, width), F32),
            jax.ShapeDtypeStruct(leaf_rows.shape, BF),
            jax.ShapeDtypeStruct((16, width), F32),
        ],
        scratch_shapes=[
            pltpu.VMEM((leaves, slots), F32),
            pltpu.VMEM((slots, width + META), BF),
            pltpu.VMEM((slots, width), F32),
        ],
        compiler_params=params(56),
        cost_estimate=cost(6 * tables * leaves * slots * width, tables * leaves * slots, 8 << 20),
        name="leaf",
    )(touched, own, other, stats, leaf_rows, cluster_rows)


def hold_kernel(*refs):
    out_ref = refs[-1]
    rows = refs[0].shape[0]
    for j, ref in enumerate(refs[:4]):
        out_ref[pl.ds(j * rows, rows), :] = ref[...]


def hold(arrays, after):
    rows, width = arrays[0].shape
    return pl.pallas_call(
        hold_kernel,
        in_specs=[pl.BlockSpec(memory_space=pltpu.VMEM)] * 4 + [pl.BlockSpec(memory_space=pl.ANY)],
        out_shape=jax.ShapeDtypeStruct((4 * rows, width), arrays[0].dtype),
        name="hold",
    )(*arrays, after)


def fetches(parts, store_ref, sems):
    step = parts[0].shape[0]
    copies = [
        pltpu.make_async_copy(part, store_ref.at[pl.ds(j * step, step)], sems.at[j])
        for j, part in enumerate(parts)
    ]
    for copy in copies:
        copy.start()
    return copies


def stored(parts):
    step, width = parts[0].shape
    return [pltpu.VMEM((step * len(parts), width), BF), pltpu.SemaphoreType.DMA((len(parts),))]


def in_hbm(count):
    return [pl.BlockSpec(memory_space=pltpu.HBM)] * count


def in_vmem(count):
    return [pl.BlockSpec(memory_space=pltpu.VMEM)] * count


def stat_kernel(*refs):
    parts, users_ref, stat_ref, store_ref, sems = refs[:8], *refs[8:]
    copies = fetches(parts, store_ref, sems)
    step = parts[0].shape[0]
    tiles = 4
    block = users_ref.shape[0] // tiles
    for tile in range(tiles):
        at = pl.ds(tile * block, block)
        users = users_ref[at, :]
        peak = total = None
        for j, copy in enumerate(copies):
            if tile == 0:
                copy.wait()
            rows = store_ref[pl.ds(j * step, step), :]
            score = lax.dot_general(rows, users, NT, preferred_element_type=F32) * LOG2E
            score = score.reshape(step // 8, 8, block)
            high = jnp.max(score, axis=0)
            if peak is None:
                peak = high
                total = jnp.sum(jnp.exp2(score - peak[None]), axis=0)
            else:
                high = jnp.maximum(peak, high)
                total = total * jnp.exp2(peak - high)
                total = total + jnp.sum(jnp.exp2(score - high[None]), axis=0)
                peak = high
        top = jnp.max(peak, axis=0, keepdims=True)
        stat_ref[0:1, at] = top
        stat_ref[1:2, at] = jnp.sum(total * jnp.exp2(peak - top), axis=0, keepdims=True)


def stat_pass(parts, users):
    step, width = parts[0].shape
    clusters, count = step * len(parts), users.shape[0]
    return pl.pallas_call(
        stat_kernel,
        in_specs=in_hbm(8) + in_vmem(1),
        out_shape=jax.ShapeDtypeStruct((2, count), F32),
        scratch_shapes=stored(parts),
        compiler_params=params(24),
        cost_estimate=cost(4 * count * clusters * width, count * clusters, 6 << 20),
        name="stats",
    )(*parts, users)


def user_kernel(*refs):
    parts, users_ref, stat_ref, out_ref, token_ref = refs[:8], *refs[8:12]
    scores, (store_ref, sems) = refs[12:14], refs[14:]
    token_ref[...] = jnp.zeros(token_ref.shape, F32)
    copies = fetches(parts, store_ref, sems)
    step = parts[0].shape[0]
    block = scores[0].shape[0]
    tiles = users_ref.shape[0] // block
    lines = block // LANES

    def score(tile):
        users = users_ref[pl.ds(tile * block, block), :]
        for j, copy in enumerate(copies):
            if tile == 0:
                copy.wait()
            at = pl.ds(j * step, step)
            scores[tile % 2][:, at] = lax.dot_general(
                users, store_ref[at, :], NT, preferred_element_type=F32
            )

    score(0)
    for tile in range(tiles):
        if tile + 1 < tiles:
            score(tile + 1)
        base = tile * block
        peak = jnp.concatenate(
            [
                jnp.broadcast_to(
                    stat_ref[0:1, base + j * LANES : base + (j + 1) * LANES], (LANES, LANES)
                ).T[:, 0:1]
                for j in range(lines)
            ],
            axis=0,
        )
        weight = jnp.exp2(scores[tile % 2][...] * LOG2E - peak).astype(BF)
        out = jnp.dot(weight, store_ref[...], preferred_element_type=F32)
        out_ref[pl.ds(base, block), :] = out.astype(BF)


def user_pass(users, stats, parts):
    count, width = users.shape
    clusters = len(parts) * parts[0].shape[0]
    block = 256
    return pl.pallas_call(
        user_kernel,
        in_specs=in_hbm(8) + in_vmem(2),
        out_shape=[
            jax.ShapeDtypeStruct((count, width), BF),
            jax.ShapeDtypeStruct((8, LANES), F32),
        ],
        scratch_shapes=[pltpu.VMEM((block, clusters), F32)] * 2 + stored(parts),
        compiler_params=params(24),
        cost_estimate=cost(4 * count * clusters * width, count * clusters, 4 << 20),
        name="user_sums",
    )(*parts, users, stats)


def cluster_kernel(place_ref, *refs):
    parts, recv_ref, users_ref = refs[:8], *refs[8:10]
    away_ref, own_ref, factor_ref = refs[11:14]
    scores, (store_ref, sems) = refs[14:16], refs[16:]
    copies = fetches(parts, store_ref, sems)
    peaks = jnp.concatenate([recv_ref[:, j, :] for j in range(8)], axis=1)
    totals = jnp.concatenate([recv_ref[:, 8 + j, :] for j in range(8)], axis=1)
    peak = jnp.max(peaks, axis=0, keepdims=True)
    total = jnp.sum(totals * jnp.exp2(peaks - peak), axis=0, keepdims=True)
    log_row = peak + jnp.log2(total)

    half = place_ref[1] * 2 + (place_ref[2] >> 1)
    mine = recv_ref[:, pl.ds(half, 1), :][:, 0, :]
    for j in range(8):
        @pl.when(half == j)
        def _():
            factor_ref[...] = jnp.exp2(mine - log_row[:, j * 256 : (j + 1) * 256])

    rows = recv_ref.shape[0]
    clusters = own_ref.shape[0]
    for dy in range(4):
        for r in range(2):
            at = clusters + (dy * 2 + r) * rows
            away_ref[pl.ds(at, rows), :] = recv_ref[:, 16 + dy * 4 + 2 + r, :].astype(BF)

    block = parts[0].shape[0]

    def score(j):
        copies[j].wait()
        scores[j % 2][...] = lax.dot_general(
            store_ref[pl.ds(j * block, block), :], users_ref[...], NT, preferred_element_type=F32
        )

    score(0)
    for j in range(len(parts)):
        if j + 1 < len(parts):
            score(j + 1)
        prob = jnp.exp2(scores[j % 2][...] * LOG2E - log_row).astype(BF)
        out = jnp.dot(prob, users_ref[...], preferred_element_type=F32)
        if j < 4:
            away_ref[pl.ds(j * block, block), :] = out.astype(BF)
        else:
            own_ref[pl.ds((j - 4) * block, block), :] = out


def cluster_pass(place, recv, users, far, near, after):
    count, width = users.shape
    parts = far + near
    block = parts[0].shape[0]
    clusters = block * 4
    peers = recv.shape[0]
    return pl.pallas_call(
        cluster_kernel,
        in_specs=[pl.BlockSpec(memory_space=pltpu.SMEM)]
        + in_hbm(8)
        + in_vmem(2)
        + [pl.BlockSpec(memory_space=pl.ANY)],
        out_shape=[
            jax.ShapeDtypeStruct((clusters + 8 * peers, width), BF),
            jax.ShapeDtypeStruct((clusters, width), F32),
            jax.ShapeDtypeStruct((peers, 2 * LANES), F32),
        ],
        scratch_shapes=[pltpu.VMEM((block, count), F32)] * 2 + stored(parts),
        compiler_params=params(28),
        cost_estimate=cost(8 * clusters * count * width, 2 * clusters * count, 8 << 20),
        name="cluster_sums",
    )(place, *parts, recv, users, after)


def both_kernel(own_ref, other_ref, recv_ref, out_ref, stay_ref, *sends):
    block = out_ref.shape[0]
    rows = recv_ref.shape[0]
    clusters = own_ref.shape[0]
    out_ref[...] = own_ref[pl.ds(0, block), :] + other_ref[pl.ds(0, block), :].astype(F32)
    for j, send in enumerate(sends):
        at = pl.ds((j + 1) * block, block)
        send[pl.ds(0, block), :] = (own_ref[at, :] + other_ref[at, :].astype(F32)).astype(BF)
    for dy in range(4):
        ref, base = (sends[3 - dy], block) if dy else (stay_ref, 0)
        for r in range(2):
            ref[pl.ds(base + r * rows, rows), :] = recv_ref[:, 16 + dy * 4 + r, :].astype(BF)
        ref[pl.ds(base + 2 * rows, 2 * rows), :] = other_ref[
            pl.ds(clusters + dy * 2 * rows, 2 * rows), :
        ]


def both_cores(own, other, recv):
    block, width = own.shape[0] // 4, own.shape[1]
    return pl.pallas_call(
        both_kernel,
        out_shape=[
            jax.ShapeDtypeStruct((block, width), F32),
            jax.ShapeDtypeStruct((64, width), BF),
        ]
        + [jax.ShapeDtypeStruct((block + 64, width), BF)] * 3,
        compiler_params=params(24),
        name="both_cores",
    )(own, other, recv)


def final_kernel(
    touched_ref, place_ref, own_ref, a_ref, b_ref, c_ref, label_ref,
    stay_ref, owner_ref, acc_ref, factor_ref, cluster_ref, user_ref,
):
    block = own_ref.shape[0]
    out = own_ref[...]
    for ref in (a_ref, b_ref, c_ref):
        out = out + ref[pl.ds(0, block), :].astype(F32)
    ids = lax.broadcasted_iota(jnp.int32, out.shape, 0)
    for k in range(2):
        out = out - jnp.where(ids == touched_ref[k], label_ref[k : k + 1, :], 0.0)
    cluster_ref[...] = out

    y, x, z, c = (place_ref[i] for i in range(4))
    users = user_ref.shape[0]
    across = jnp.broadcast_to(owner_ref[...], (users, users))
    rows = lax.broadcasted_iota(jnp.int32, (users, users), 0)
    cols = lax.broadcasted_iota(jnp.int32, (users, users), 1)
    down = jnp.sum(jnp.where(rows == cols, across, 0), axis=1, keepdims=True)
    rank = jnp.sum(((across == down) & (rows < cols)).astype(jnp.int32), axis=0, keepdims=True)
    line = lax.broadcasted_iota(jnp.int32, (256, users), 0)
    target = ((y + (line >> 6)) & 3) * 32 + (line & 15) * 2 + (c ^ ((line >> 5) & 1))
    pick = (target == owner_ref[...]) & (((line >> 4) & 1) == rank)
    pick = pick.astype(F32).astype(BF)
    leaf = jnp.concatenate(
        [stay_ref[...]] + [ref[pl.ds(block, 64), :] for ref in (c_ref, b_ref, a_ref)], axis=0
    )
    out = lax.dot_general(pick, leaf, TN, preferred_element_type=F32)
    odd = (place_ref[2] & 1) == 1
    factor = jnp.where(odd, factor_ref[:, LANES:], factor_ref[:, :LANES]).T
    for q in range(acc_ref.shape[0]):
        out = out + acc_ref[q].astype(F32) * factor[:, q : q + 1]
    user_ref[...] = out


def final_pass(touched, place, own, arrived, labels, stay, owner, acc, factor):
    return pl.pallas_call(
        final_kernel,
        in_specs=[pl.BlockSpec(memory_space=pltpu.SMEM)] * 2
        + [pl.BlockSpec(memory_space=pltpu.VMEM)] * 9,
        out_shape=[
            jax.ShapeDtypeStruct(own.shape, F32),
            jax.ShapeDtypeStruct(acc.shape[1:], F32),
        ],
        compiler_params=params(24),
        name="final",
    )(touched, place, own, *arrived, labels, stay, owner[None], acc, factor)


def shift(x, axis, by):
    size = lax.axis_size(axis)
    return lax.ppermute(x, axis, [(i, (i + by) % size) for i in range(size)])


def swap(x, axis):
    return lax.all_to_all(x, axis, 0, 0, tiled=True)


def per_device(user_vec, cluster_rows, leaf_rows, touched, route_owner, route_slot, leaf_label):
    peers = lax.axis_size(PLANE)
    count, width = user_vec.shape
    hops = range(1, 4)
    place = jnp.stack([lax.axis_index(name) for name in ALL]).astype(jnp.int32)

    ready = prep(user_vec, route_owner, route_slot, leaf_label)
    near = [cluster_rows] + [shift(cluster_rows, "y", -j) for j in hops]
    plane = swap(ready, PLANE)
    far = [shift(part, "c", 1) for part in near]

    users, _, *sends = select_pass(place, plane)
    came = [sends[0]] + [shift(sends[j], "y", j) for j in hops]
    mine = stat_pass(near + far, users)
    came = hold(came, mine)
    cross = shift(came, "c", 1)
    back, leaf_grad, labels = leaf_pass(touched, came, cross, mine, leaf_rows, cluster_rows)
    recv = swap(back, PLANE)
    acc, token = user_pass(users, mine, near + far)

    away, own, factor = cluster_pass(place, recv, users, far, near, token)
    away = shift(away, "c", 1)
    acc = swap(acc.reshape(peers, count, width), PLANE)
    own, stay, *sends = both_cores(own, away, recv)
    arrived = [shift(x, "y", j) for j, x in zip(hops, sends)]
    cluster_grad, user_grad = final_pass(
        touched, place, own, arrived, labels, stay, route_owner, acc, factor
    )
    return user_grad, cluster_grad, leaf_grad


def solution(mesh):
    grid = Mesh(mesh.devices.reshape(4, 4, 4, 2), ALL)
    one = P(ALL)
    return jax.shard_map(
        per_device,
        mesh=grid,
        in_specs=(P(ALL, None), P(ALL, None), P(ALL, None, None), one, one, one, one),
        out_specs=(P(ALL, None), P(ALL, None), P(ALL, None, None)),
        check_vma=False,
    )
```

```python
import jax
import jax.numpy as jnp
from jax import lax
from jax.experimental import pallas as pl
from jax.experimental.pallas import tpu as pltpu
from jax.sharding import Mesh
from jax.sharding import PartitionSpec as P

BF = jnp.bfloat16
F32 = jnp.float32
LOG2E = 1.4426950408889634
ALL = ("y", "x", "z", "c")
PLANE = ("x", "z")
NT = (((1,), (1,)), ((), ()))
TN = (((0,), (0,)), ((), ()))
META = 128
EXTRA = 16
LANES = 128


def params(mib):
    return pltpu.CompilerParams(vmem_limit_bytes=mib << 20)


def little():
    return pl.CostEstimate(flops=1, transcendentals=0, bytes_accessed=1)


def whole(shape):
    return pl.BlockSpec(shape, lambda *ids: (0,) * len(shape))


def prep_kernel(user_ref, owner_ref, slot_ref, leaf_ref, out_ref):
    count, width = user_ref.shape
    for j in range(out_ref.shape[0]):
        out_ref[j, :count, :] = user_ref[...]
    line = lax.broadcasted_iota(jnp.int32, (EXTRA, count), 0)
    leaf = leaf_ref[...]
    left = jnp.where(line == 0, owner_ref[...], jnp.where(line == 1, leaf >> 6, 0))
    right = jnp.where(line == 0, slot_ref[...] + 1, jnp.where(line == 1, leaf & 63, 0))
    both = jnp.concatenate([left, right], axis=1)
    for j in range(out_ref.shape[0]):
        out_ref[j, count:, :] = both.astype(F32).astype(BF)


def prep(user_vec, owner, slot, leaf):
    count, width = user_vec.shape
    return pl.pallas_call(
        prep_kernel,
        out_shape=jax.ShapeDtypeStruct((16, count + EXTRA, width), BF),
        name="prep",
    )(user_vec, owner[None], slot[None], leaf[None])


def select_kernel(place_ref, plane_ref, *refs):
    users_ref, pick_ref = refs[:2]
    send_ref = refs[2]
    owner_ref, slot_ref, high_ref, low_ref, rows_ref = refs[3:]
    count = LANES
    width = users_ref.shape[1]
    homes = users_ref.shape[0] // count
    y, x, z, c = (place_ref[i] for i in range(4))
    for home in range(homes):
        users_ref[pl.ds(home * count, count), :] = plane_ref[home, :count, :]
        extra = plane_ref[home, count:, :].astype(F32)
        at = pl.ds(home, 1)
        owner_ref[at, :] = extra[0:1, :count]
        slot_ref[at, :] = extra[0:1, count:]
        high_ref[at, :] = extra[1:2, :count]
        low_ref[at, :] = extra[1:2, count:]

    line = lax.broadcasted_iota(jnp.int32, (8, count), 0)
    target = ((y + (line & 3)) & 3) * 32 + x * 8 + z * 2 + (c ^ (line >> 2))
    target = target.astype(F32)
    match = jnp.concatenate(
        [
            (jnp.broadcast_to(owner_ref[h : h + 1, :], (8, count)) == target).astype(F32)
            for h in range(homes)
        ],
        axis=0,
    )
    rows = lax.broadcasted_iota(jnp.int32, (count, count), 0)
    cols = lax.broadcasted_iota(jnp.int32, (count, count), 1)
    before = (rows < cols).astype(F32).astype(BF)
    rank = jnp.dot(match.astype(BF), before, preferred_element_type=F32)
    first = match * (rank == 0.0).astype(F32)
    second = match * (rank == 1.0).astype(F32)
    lines = lax.broadcasted_iota(jnp.int32, (LANES, count), 0)
    for h in range(homes):
        part = slice(h * 8, (h + 1) * 8)
        pick = jnp.concatenate([first[part], second[part]], axis=0).astype(BF)
        pick_ref[pl.ds(h * 16, 16), :] = pick
        rows_ref[h, :, :width] = jnp.dot(
            pick, users_ref[pl.ds(h * count, count), :], preferred_element_type=F32
        )
        meta = jnp.where(lines == 0, slot_ref[h : h + 1, :], 0.0)
        meta = jnp.where(lines == 1, high_ref[h : h + 1, :], meta)
        meta = jnp.where(lines == 2, low_ref[h : h + 1, :], meta)
        rows_ref[h, :, width:] = lax.dot_general(
            pick, meta.astype(BF), NT, preferred_element_type=F32
        )
    for dy in range(4):
        for core in range(2):
            there = ((y + dy) & 3) * 2 + (c ^ core)
            for r in range(2):
                send_ref[there, pl.ds(r * 16, 16), :] = rows_ref[
                    :, r * 8 + core * 4 + dy, :
                ].astype(BF)


def select_pass(place, plane):
    homes, _, width = plane.shape
    users = homes * LANES
    return pl.pallas_call(
        select_kernel,
        in_specs=[pl.BlockSpec(memory_space=pltpu.SMEM)]
        + [pl.BlockSpec(memory_space=pltpu.VMEM)],
        out_shape=[
            jax.ShapeDtypeStruct((users, width), BF),
            jax.ShapeDtypeStruct((homes * 16, LANES), BF),
            jax.ShapeDtypeStruct((8, 32, width + META), BF),
        ],
        scratch_shapes=[pltpu.VMEM((homes, LANES), F32)] * 4
        + [pltpu.VMEM((homes, 16, width + META), F32)],
        compiler_params=params(16),
        name="select",
    )(place, plane)


def leaf_kernel(*refs):
    touched_ref, place_ref, came_ref, stat_ref, table_ref, cluster_ref = refs[:6]
    back_ref, grad_ref, label_ref, score_ref, recv_ref, part_ref = refs[6:]
    k = pl.program_id(0)
    slots, width = part_ref.shape

    @pl.when(k == 0)
    def _():
        for dy in range(4):
            for core in range(2):
                home = ((place_ref[0] - dy) & 3) * 2 + (place_ref[3] ^ core)
                recv_ref[pl.ds(dy * 64 + core * 32, 32), :] = came_ref[home]

    leaves = table_ref.shape[1]
    step = 512
    users = recv_ref[:, :width]
    meta = recv_ref[:, width:].astype(F32).T
    slot = meta[0:1, :] - 1.0
    leaf = (meta[1:2, :] * 64.0 + meta[2:3, :]).astype(jnp.int32)
    chosen = slot == k.astype(F32)
    leaf = jnp.where(chosen, leaf, -1)

    @pl.when(k == 0)
    def _():
        line = lax.broadcasted_iota(jnp.int32, (16, slots), 0)
        mine = (jnp.broadcast_to(slot, (16, slots)) == line.astype(F32)).astype(F32).astype(BF)
        label_ref[...] = jnp.dot(mine, users, preferred_element_type=F32)
        clusters = cluster_ref.shape[0]
        line = lax.broadcasted_iota(jnp.int32, (16, clusters), 0)
        column = lax.broadcasted_iota(jnp.int32, (16, clusters), 1)
        target = jnp.where(line == 0, touched_ref[0], jnp.where(line == 1, touched_ref[1], -1))
        pick = (column == target).astype(F32).astype(BF)
        rows = jnp.dot(pick, cluster_ref[...], preferred_element_type=F32).astype(BF)
        part_ref[...] = -lax.dot_general(mine, rows, TN, preferred_element_type=F32)

    peak = None
    for j in range(leaves // step):
        score = lax.dot_general(
            table_ref[0, pl.ds(j * step, step), :], users, NT, preferred_element_type=F32
        )
        score_ref[pl.ds(j * step, step), :] = score
        high = jnp.max(score.reshape(step // 8, 8, slots), axis=0)
        peak = high if peak is None else jnp.maximum(peak, high)
    peak = jnp.max(peak, axis=0, keepdims=True) * LOG2E
    total = jnp.zeros((8, slots), F32)
    for j in range(leaves // step):
        weight = jnp.exp2(score_ref[pl.ds(j * step, step), :] * LOG2E - peak)
        score_ref[pl.ds(j * step, step), :] = weight
        total = total + jnp.sum(weight.reshape(step // 8, 8, slots), axis=0)
    scale = chosen.astype(F32) / jnp.sum(total, axis=0, keepdims=True)
    part = jnp.zeros((slots, width), F32)
    for j in range(leaves // step):
        ids = lax.broadcasted_iota(jnp.int32, (step, slots), 0) + j * step
        coef = score_ref[pl.ds(j * step, step), :] * scale - (ids == leaf).astype(F32)
        coef = coef.astype(BF)
        grad_ref[0, pl.ds(j * step, step), :] = jnp.dot(
            coef, users, preferred_element_type=F32
        ).astype(BF)
        part = part + lax.dot_general(
            coef, table_ref[0, pl.ds(j * step, step), :], TN, preferred_element_type=F32
        )
    part_ref[...] += part

    @pl.when(k == pl.num_programs(0) - 1)
    def _():
        peers = back_ref.shape[0]
        for j in range(8):
            at = slice(j * width, (j + 1) * width)
            back_ref[:, j, :] = jnp.broadcast_to(stat_ref[0:1, at], (peers, width))
            back_ref[:, 8 + j, :] = jnp.broadcast_to(stat_ref[1:2, at], (peers, width))
        for j in range(16):
            back_ref[:, 16 + j, :] = part_ref[pl.ds(j * peers, peers), :]


def leaf_pass(touched, place, came, stats, leaf_rows, cluster_rows):
    tables, leaves, width = leaf_rows.shape
    slots = came.shape[0] * came.shape[1]
    peers = slots // 16
    return pl.pallas_call(
        leaf_kernel,
        grid=(tables,),
        in_specs=[
            pl.BlockSpec(memory_space=pltpu.SMEM),
            pl.BlockSpec(memory_space=pltpu.SMEM),
            whole(came.shape),
            whole(stats.shape),
            pl.BlockSpec((1, leaves, width), lambda k: (k, 0, 0)),
            whole(cluster_rows.shape),
        ],
        out_specs=[
            whole((peers, 32, width)),
            pl.BlockSpec((1, leaves, width), lambda k: (k, 0, 0)),
            whole((16, width)),
        ],
        out_shape=[
            jax.ShapeDtypeStruct((peers, 32, width), F32),
            jax.ShapeDtypeStruct(leaf_rows.shape, BF),
            jax.ShapeDtypeStruct((16, width), F32),
        ],
        scratch_shapes=[
            pltpu.VMEM((leaves, slots), F32),
            pltpu.VMEM((slots, width + META), BF),
            pltpu.VMEM((slots, width), F32),
        ],
        compiler_params=params(56),
        cost_estimate=little(),
        name="leaf",
    )(touched, place, came, stats, leaf_rows, cluster_rows)


def fetches(parts, store_ref, sems):
    step = parts[0].shape[0]
    copies = [
        pltpu.make_async_copy(part, store_ref.at[pl.ds(j * step, step)], sems.at[j])
        for j, part in enumerate(parts)
    ]
    for copy in copies:
        copy.start()
    return copies


def stored(parts):
    step, width = parts[0].shape
    return [pltpu.VMEM((step * len(parts), width), BF), pltpu.SemaphoreType.DMA((len(parts),))]


def in_hbm(count):
    return [pl.BlockSpec(memory_space=pltpu.HBM)] * count


def in_vmem(count):
    return [pl.BlockSpec(memory_space=pltpu.VMEM)] * count


def stat_kernel(*refs):
    parts, users_ref, stat_ref, store_ref, sems = refs[:8], *refs[8:]
    copies = fetches(parts, store_ref, sems)
    step = parts[0].shape[0]
    tiles = 4
    block = users_ref.shape[0] // tiles
    for tile in range(tiles):
        at = pl.ds(tile * block, block)
        users = users_ref[at, :]
        peak = total = None
        for j, copy in enumerate(copies):
            if tile == 0:
                copy.wait()
            rows = store_ref[pl.ds(j * step, step), :]
            score = lax.dot_general(rows, users, NT, preferred_element_type=F32) * LOG2E
            score = score.reshape(step // 8, 8, block)
            high = jnp.max(score, axis=0)
            if peak is None:
                peak = high
                total = jnp.sum(jnp.exp2(score - peak[None]), axis=0)
            else:
                high = jnp.maximum(peak, high)
                total = total * jnp.exp2(peak - high)
                total = total + jnp.sum(jnp.exp2(score - high[None]), axis=0)
                peak = high
        top = jnp.max(peak, axis=0, keepdims=True)
        stat_ref[0:1, at] = top
        stat_ref[1:2, at] = jnp.sum(total * jnp.exp2(peak - top), axis=0, keepdims=True)


def stat_pass(parts, users):
    step, width = parts[0].shape
    clusters, count = step * len(parts), users.shape[0]
    return pl.pallas_call(
        stat_kernel,
        in_specs=in_hbm(8) + in_vmem(1),
        out_shape=jax.ShapeDtypeStruct((2, count), F32),
        scratch_shapes=stored(parts),
        compiler_params=params(24),
        cost_estimate=little(),
        name="stats",
    )(*parts, users)


def user_kernel(*refs):
    parts, users_ref, stat_ref, out_ref, token_ref = refs[:8], *refs[8:12]
    scores, (store_ref, sems) = refs[12:14], refs[14:]
    token_ref[...] = jnp.zeros(token_ref.shape, F32)
    copies = fetches(parts, store_ref, sems)
    step = parts[0].shape[0]
    block = scores[0].shape[0]
    tiles = users_ref.shape[0] // block
    lines = block // LANES

    def score(tile):
        users = users_ref[pl.ds(tile * block, block), :]
        for j, copy in enumerate(copies):
            if tile == 0:
                copy.wait()
            at = pl.ds(j * step, step)
            scores[tile % 2][:, at] = lax.dot_general(
                users, store_ref[at, :], NT, preferred_element_type=F32
            )

    score(0)
    for tile in range(tiles):
        if tile + 1 < tiles:
            score(tile + 1)
        base = tile * block
        peak = jnp.concatenate(
            [
                jnp.broadcast_to(
                    stat_ref[0:1, base + j * LANES : base + (j + 1) * LANES], (LANES, LANES)
                ).T[:, 0:1]
                for j in range(lines)
            ],
            axis=0,
        )
        weight = jnp.exp2(scores[tile % 2][...] * LOG2E - peak).astype(BF)
        out = jnp.dot(weight, store_ref[...], preferred_element_type=F32)
        out_ref[pl.ds(base, block), :] = out.astype(BF)


def user_pass(users, stats, parts):
    count, width = users.shape
    clusters = len(parts) * parts[0].shape[0]
    block = 256
    return pl.pallas_call(
        user_kernel,
        in_specs=in_hbm(8) + in_vmem(2),
        out_shape=[
            jax.ShapeDtypeStruct((count, width), BF),
            jax.ShapeDtypeStruct((8, LANES), F32),
        ],
        scratch_shapes=[pltpu.VMEM((block, clusters), F32)] * 2 + stored(parts),
        compiler_params=params(24),
        cost_estimate=little(),
        name="user_sums",
    )(*parts, users, stats)


def cluster_kernel(place_ref, *refs):
    parts, recv_ref, users_ref = refs[:8], *refs[8:10]
    away_ref, own_ref, factor_ref = refs[11:14]
    scores, (store_ref, sems) = refs[14:16], refs[16:]
    copies = fetches(parts, store_ref, sems)
    peaks = jnp.concatenate([recv_ref[:, j, :] for j in range(8)], axis=1)
    totals = jnp.concatenate([recv_ref[:, 8 + j, :] for j in range(8)], axis=1)
    peak = jnp.max(peaks, axis=0, keepdims=True)
    total = jnp.sum(totals * jnp.exp2(peaks - peak), axis=0, keepdims=True)
    log_row = peak + jnp.log2(total)

    half = place_ref[1] * 2 + (place_ref[2] >> 1)
    mine = recv_ref[:, pl.ds(half, 1), :][:, 0, :]
    for j in range(8):
        @pl.when(half == j)
        def _():
            factor_ref[...] = jnp.exp2(mine - log_row[:, j * 256 : (j + 1) * 256])

    rows = recv_ref.shape[0]
    clusters = own_ref.shape[0]
    for dy in range(4):
        for r in range(2):
            at = clusters + (dy * 2 + r) * rows
            away_ref[pl.ds(at, rows), :] = recv_ref[:, 16 + dy * 4 + 2 + r, :].astype(BF)

    block = parts[0].shape[0]

    def score(j):
        copies[j].wait()
        scores[j % 2][...] = lax.dot_general(
            store_ref[pl.ds(j * block, block), :], users_ref[...], NT, preferred_element_type=F32
        )

    score(0)
    for j in range(len(parts)):
        if j + 1 < len(parts):
            score(j + 1)
        prob = jnp.exp2(scores[j % 2][...] * LOG2E - log_row).astype(BF)
        out = jnp.dot(prob, users_ref[...], preferred_element_type=F32)
        if j < 4:
            away_ref[pl.ds(j * block, block), :] = out.astype(BF)
        else:
            own_ref[pl.ds((j - 4) * block, block), :] = out.astype(BF)


def cluster_pass(place, recv, users, far, near, after):
    count, width = users.shape
    parts = far + near
    block = parts[0].shape[0]
    clusters = block * 4
    peers = recv.shape[0]
    return pl.pallas_call(
        cluster_kernel,
        in_specs=[pl.BlockSpec(memory_space=pltpu.SMEM)]
        + in_hbm(8)
        + in_vmem(2)
        + [pl.BlockSpec(memory_space=pl.ANY)],
        out_shape=[
            jax.ShapeDtypeStruct((clusters + 8 * peers, width), BF),
            jax.ShapeDtypeStruct((clusters, width), BF),
            jax.ShapeDtypeStruct((peers, 2 * LANES), F32),
        ],
        scratch_shapes=[pltpu.VMEM((block, count), F32)] * 2 + stored(parts),
        compiler_params=params(28),
        cost_estimate=little(),
        name="cluster_sums",
    )(place, *parts, recv, users, after)


def both_kernel(own_ref, other_ref, recv_ref, out_ref, stay_ref, *sends):
    block = out_ref.shape[0]
    rows = recv_ref.shape[0]
    clusters = own_ref.shape[0]
    out_ref[...] = own_ref[pl.ds(0, block), :].astype(F32) + other_ref[pl.ds(0, block), :].astype(F32)
    for j, send in enumerate(sends):
        at = pl.ds((j + 1) * block, block)
        send[pl.ds(0, block), :] = (own_ref[at, :].astype(F32) + other_ref[at, :].astype(F32)).astype(BF)
    for dy in range(4):
        ref, base = (sends[3 - dy], block) if dy else (stay_ref, 0)
        for r in range(2):
            ref[pl.ds(base + r * rows, rows), :] = recv_ref[:, 16 + dy * 4 + r, :].astype(BF)
        ref[pl.ds(base + 2 * rows, 2 * rows), :] = other_ref[
            pl.ds(clusters + dy * 2 * rows, 2 * rows), :
        ]


def both_cores(own, other, recv):
    block, width = own.shape[0] // 4, own.shape[1]
    return pl.pallas_call(
        both_kernel,
        out_shape=[
            jax.ShapeDtypeStruct((block, width), F32),
            jax.ShapeDtypeStruct((64, width), BF),
        ]
        + [jax.ShapeDtypeStruct((block + 64, width), BF)] * 3,
        compiler_params=params(24),
        name="both_cores",
    )(own, other, recv)


def final_kernel(
    touched_ref, place_ref, own_ref, a_ref, b_ref, c_ref, label_ref,
    stay_ref, owner_ref, acc_ref, factor_ref, cluster_ref, user_ref,
):
    block = own_ref.shape[0]
    out = own_ref[...]
    for ref in (a_ref, b_ref, c_ref):
        out = out + ref[pl.ds(0, block), :].astype(F32)
    ids = lax.broadcasted_iota(jnp.int32, out.shape, 0)
    for k in range(2):
        out = out - jnp.where(ids == touched_ref[k], label_ref[k : k + 1, :], 0.0)
    cluster_ref[...] = out

    y, x, z, c = (place_ref[i] for i in range(4))
    users = user_ref.shape[0]
    across = jnp.broadcast_to(owner_ref[...], (users, users))
    rows = lax.broadcasted_iota(jnp.int32, (users, users), 0)
    cols = lax.broadcasted_iota(jnp.int32, (users, users), 1)
    down = jnp.sum(jnp.where(rows == cols, across, 0), axis=1, keepdims=True)
    rank = jnp.sum(((across == down) & (rows < cols)).astype(jnp.int32), axis=0, keepdims=True)
    line = lax.broadcasted_iota(jnp.int32, (256, users), 0)
    target = ((y + (line >> 6)) & 3) * 32 + (line & 15) * 2 + (c ^ ((line >> 5) & 1))
    pick = (target == owner_ref[...]) & (((line >> 4) & 1) == rank)
    pick = pick.astype(F32).astype(BF)
    leaf = jnp.concatenate(
        [stay_ref[...]] + [ref[pl.ds(block, 64), :] for ref in (c_ref, b_ref, a_ref)], axis=0
    )
    out = lax.dot_general(pick, leaf, TN, preferred_element_type=F32)
    odd = (place_ref[2] & 1) == 1
    factor = jnp.where(odd, factor_ref[:, LANES:], factor_ref[:, :LANES]).T
    for q in range(acc_ref.shape[0]):
        out = out + acc_ref[q].astype(F32) * factor[:, q : q + 1]
    user_ref[...] = out


def final_pass(touched, place, own, arrived, labels, stay, owner, acc, factor):
    return pl.pallas_call(
        final_kernel,
        in_specs=[pl.BlockSpec(memory_space=pltpu.SMEM)] * 2
        + [pl.BlockSpec(memory_space=pltpu.VMEM)] * 9,
        out_shape=[
            jax.ShapeDtypeStruct(own.shape, F32),
            jax.ShapeDtypeStruct(acc.shape[1:], F32),
        ],
        compiler_params=params(24),
        name="final",
    )(touched, place, own, *arrived, labels, stay, owner[None], acc, factor)


def shift(x, axis, by):
    size = lax.axis_size(axis)
    return lax.ppermute(x, axis, [(i, (i + by) % size) for i in range(size)])


def swap(x, axis):
    return lax.all_to_all(x, axis, 0, 0, tiled=True)


def per_device(user_vec, cluster_rows, leaf_rows, touched, route_owner, route_slot, leaf_label):
    peers = lax.axis_size(PLANE)
    count, width = user_vec.shape
    hops = range(1, 4)
    place = jnp.stack([lax.axis_index(name) for name in ALL]).astype(jnp.int32)

    ready = prep(user_vec, route_owner, route_slot, leaf_label)
    near = [cluster_rows] + [shift(cluster_rows, "y", -j) for j in hops]
    plane = swap(ready, PLANE)
    far = [shift(part, "c", 1) for part in near]

    users, _, sends = select_pass(place, plane)
    came = swap(sends, ("y", "c"))
    mine = stat_pass(near + far, users)
    back, leaf_grad, labels = leaf_pass(touched, place, came, mine, leaf_rows, cluster_rows)
    recv = swap(back, PLANE)
    acc, token = user_pass(users, mine, near + far)

    away, own, factor = cluster_pass(place, recv, users, far, near, token)
    away = shift(away, "c", 1)
    acc = swap(acc.reshape(peers, count, width), PLANE)
    own, stay, *sends = both_cores(own, away, recv)
    arrived = [shift(x, "y", j) for j, x in zip(hops, sends)]
    cluster_grad, user_grad = final_pass(
        touched, place, own, arrived, labels, stay, route_owner, acc, factor
    )
    return user_grad, cluster_grad, leaf_grad


def solution(mesh):
    grid = Mesh(mesh.devices.reshape(4, 4, 4, 2), ALL)
    one = P(ALL)
    return jax.shard_map(
        per_device,
        mesh=grid,
        in_specs=(P(ALL, None), P(ALL, None), P(ALL, None, None), one, one, one, one),
        out_specs=(P(ALL, None), P(ALL, None), P(ALL, None, None)),
        check_vma=False,
    )
```

```python
import jax
import jax.numpy as jnp
from jax import lax
from jax.experimental import pallas as pl
from jax.experimental.pallas import tpu as pltpu
from jax.sharding import Mesh
from jax.sharding import PartitionSpec as P

BF = jnp.bfloat16
F32 = jnp.float32
LOG2E = 1.4426950408889634
ALL = ("y", "x", "z", "c")
PLANE = ("x", "z")
NT = (((1,), (1,)), ((), ()))
TN = (((0,), (0,)), ((), ()))
META = 128
EXTRA = 16
STEPS = (1, 3, 2)
ARRIVE = (2, 1, 3)
LANES = 128


def params(mib):
    return pltpu.CompilerParams(vmem_limit_bytes=mib << 20)


def little():
    return pl.CostEstimate(flops=1, transcendentals=0, bytes_accessed=1)


def whole(shape):
    return pl.BlockSpec(shape, lambda *ids: (0,) * len(shape))


def prep_kernel(user_ref, owner_ref, slot_ref, leaf_ref, out_ref):
    count, width = user_ref.shape
    for j in range(out_ref.shape[0]):
        out_ref[j, :count, :] = user_ref[...]
    line = lax.broadcasted_iota(jnp.int32, (EXTRA, count), 0)
    leaf = leaf_ref[...]
    left = jnp.where(line == 0, owner_ref[...], jnp.where(line == 1, leaf >> 6, 0))
    right = jnp.where(line == 0, slot_ref[...] + 1, jnp.where(line == 1, leaf & 63, 0))
    both = jnp.concatenate([left, right], axis=1)
    for j in range(out_ref.shape[0]):
        out_ref[j, count:, :] = both.astype(F32).astype(BF)


def prep(user_vec, owner, slot, leaf):
    count, width = user_vec.shape
    return pl.pallas_call(
        prep_kernel,
        out_shape=jax.ShapeDtypeStruct((16, count + EXTRA, width), BF),
        name="prep",
    )(user_vec, owner[None], slot[None], leaf[None])


def select_kernel(place_ref, plane_ref, *refs):
    users_ref, pick_ref = refs[:2]
    send_ref = refs[2]
    owner_ref, slot_ref, high_ref, low_ref, rows_ref = refs[3:]
    count = LANES
    width = users_ref.shape[1]
    homes = users_ref.shape[0] // count
    y, x, z, c = (place_ref[i] for i in range(4))
    for home in range(homes):
        users_ref[pl.ds(home * count, count), :] = plane_ref[home, :count, :]
        extra = plane_ref[home, count:, :].astype(F32)
        at = pl.ds(home, 1)
        owner_ref[at, :] = extra[0:1, :count]
        slot_ref[at, :] = extra[0:1, count:]
        high_ref[at, :] = extra[1:2, :count]
        low_ref[at, :] = extra[1:2, count:]

    line = lax.broadcasted_iota(jnp.int32, (8, count), 0)
    target = ((y + (line & 3)) & 3) * 32 + x * 8 + z * 2 + (c ^ (line >> 2))
    target = target.astype(F32)
    match = jnp.concatenate(
        [
            (jnp.broadcast_to(owner_ref[h : h + 1, :], (8, count)) == target).astype(F32)
            for h in range(homes)
        ],
        axis=0,
    )
    rows = lax.broadcasted_iota(jnp.int32, (count, count), 0)
    cols = lax.broadcasted_iota(jnp.int32, (count, count), 1)
    before = (rows < cols).astype(F32).astype(BF)
    rank = jnp.dot(match.astype(BF), before, preferred_element_type=F32)
    first = match * (rank == 0.0).astype(F32)
    second = match * (rank == 1.0).astype(F32)
    lines = lax.broadcasted_iota(jnp.int32, (LANES, count), 0)
    for h in range(homes):
        part = slice(h * 8, (h + 1) * 8)
        pick = jnp.concatenate([first[part], second[part]], axis=0).astype(BF)
        pick_ref[pl.ds(h * 16, 16), :] = pick
        rows_ref[h, :, :width] = jnp.dot(
            pick, users_ref[pl.ds(h * count, count), :], preferred_element_type=F32
        )
        meta = jnp.where(lines == 0, slot_ref[h : h + 1, :], 0.0)
        meta = jnp.where(lines == 1, high_ref[h : h + 1, :], meta)
        meta = jnp.where(lines == 2, low_ref[h : h + 1, :], meta)
        rows_ref[h, :, width:] = lax.dot_general(
            pick, meta.astype(BF), NT, preferred_element_type=F32
        )
    for dy in range(4):
        for core in range(2):
            there = ((y + dy) & 3) * 2 + (c ^ core)
            for r in range(2):
                send_ref[there, pl.ds(r * 16, 16), :] = rows_ref[
                    :, r * 8 + core * 4 + dy, :
                ].astype(BF)


def select_pass(place, plane):
    homes, _, width = plane.shape
    users = homes * LANES
    return pl.pallas_call(
        select_kernel,
        in_specs=[pl.BlockSpec(memory_space=pltpu.SMEM)]
        + [pl.BlockSpec(memory_space=pltpu.VMEM)],
        out_shape=[
            jax.ShapeDtypeStruct((users, width), BF),
            jax.ShapeDtypeStruct((homes * 16, LANES), BF),
            jax.ShapeDtypeStruct((8, 32, width + META), BF),
        ],
        scratch_shapes=[pltpu.VMEM((homes, LANES), F32)] * 4
        + [pltpu.VMEM((homes, 16, width + META), F32)],
        compiler_params=params(16),
        name="select",
    )(place, plane)


def leaf_kernel(*refs):
    touched_ref, place_ref, came_ref, stat_ref, table_ref, cluster_ref = refs[:6]
    back_ref, grad_ref, label_ref, score_ref, recv_ref, part_ref = refs[6:]
    k = pl.program_id(0)
    slots, width = part_ref.shape

    @pl.when(k == 0)
    def _():
        for dy in range(4):
            for core in range(2):
                home = ((place_ref[0] - dy) & 3) * 2 + (place_ref[3] ^ core)
                recv_ref[pl.ds(dy * 64 + core * 32, 32), :] = came_ref[home]

    leaves = table_ref.shape[1]
    step = 512
    users = recv_ref[:, :width]
    meta = recv_ref[:, width:].astype(F32).T
    slot = meta[0:1, :] - 1.0
    leaf = (meta[1:2, :] * 64.0 + meta[2:3, :]).astype(jnp.int32)
    chosen = slot == k.astype(F32)
    leaf = jnp.where(chosen, leaf, -1)

    @pl.when(k == 0)
    def _():
        line = lax.broadcasted_iota(jnp.int32, (16, slots), 0)
        mine = (jnp.broadcast_to(slot, (16, slots)) == line.astype(F32)).astype(F32).astype(BF)
        label_ref[...] = jnp.dot(mine, users, preferred_element_type=F32)
        clusters = cluster_ref.shape[0]
        line = lax.broadcasted_iota(jnp.int32, (16, clusters), 0)
        column = lax.broadcasted_iota(jnp.int32, (16, clusters), 1)
        target = jnp.where(line == 0, touched_ref[0], jnp.where(line == 1, touched_ref[1], -1))
        pick = (column == target).astype(F32).astype(BF)
        rows = jnp.dot(pick, cluster_ref[...], preferred_element_type=F32).astype(BF)
        part_ref[...] = -lax.dot_general(mine, rows, TN, preferred_element_type=F32)

    peak = None
    for j in range(leaves // step):
        score = lax.dot_general(
            table_ref[0, pl.ds(j * step, step), :], users, NT, preferred_element_type=F32
        )
        score_ref[pl.ds(j * step, step), :] = score
        high = jnp.max(score.reshape(step // 8, 8, slots), axis=0)
        peak = high if peak is None else jnp.maximum(peak, high)
    peak = jnp.max(peak, axis=0, keepdims=True) * LOG2E
    total = jnp.zeros((8, slots), F32)
    for j in range(leaves // step):
        weight = jnp.exp2(score_ref[pl.ds(j * step, step), :] * LOG2E - peak)
        score_ref[pl.ds(j * step, step), :] = weight
        total = total + jnp.sum(weight.reshape(step // 8, 8, slots), axis=0)
    scale = chosen.astype(F32) / jnp.sum(total, axis=0, keepdims=True)
    part = jnp.zeros((slots, width), F32)
    for j in range(leaves // step):
        ids = lax.broadcasted_iota(jnp.int32, (step, slots), 0) + j * step
        coef = score_ref[pl.ds(j * step, step), :] * scale - (ids == leaf).astype(F32)
        coef = coef.astype(BF)
        grad_ref[0, pl.ds(j * step, step), :] = jnp.dot(
            coef, users, preferred_element_type=F32
        ).astype(BF)
        part = part + lax.dot_general(
            coef, table_ref[0, pl.ds(j * step, step), :], TN, preferred_element_type=F32
        )
    part_ref[...] += part

    @pl.when(k == pl.num_programs(0) - 1)
    def _():
        peers = back_ref.shape[0]
        for j in range(8):
            at = slice(j * width, (j + 1) * width)
            back_ref[:, j, :] = jnp.broadcast_to(stat_ref[0:1, at], (peers, width))
            back_ref[:, 8 + j, :] = jnp.broadcast_to(stat_ref[1:2, at], (peers, width))
        for j in range(16):
            back_ref[:, 16 + j, :] = part_ref[pl.ds(j * peers, peers), :]


def leaf_pass(touched, place, came, stats, leaf_rows, cluster_rows):
    tables, leaves, width = leaf_rows.shape
    slots = came.shape[0] * came.shape[1]
    peers = slots // 16
    return pl.pallas_call(
        leaf_kernel,
        grid=(tables,),
        in_specs=[
            pl.BlockSpec(memory_space=pltpu.SMEM),
            pl.BlockSpec(memory_space=pltpu.SMEM),
            whole(came.shape),
            whole(stats.shape),
            pl.BlockSpec((1, leaves, width), lambda k: (k, 0, 0)),
            whole(cluster_rows.shape),
        ],
        out_specs=[
            whole((peers, 32, width)),
            pl.BlockSpec((1, leaves, width), lambda k: (k, 0, 0)),
            whole((16, width)),
        ],
        out_shape=[
            jax.ShapeDtypeStruct((peers, 32, width), F32),
            jax.ShapeDtypeStruct(leaf_rows.shape, BF),
            jax.ShapeDtypeStruct((16, width), F32),
        ],
        scratch_shapes=[
            pltpu.VMEM((leaves, slots), F32),
            pltpu.VMEM((slots, width + META), BF),
            pltpu.VMEM((slots, width), F32),
        ],
        compiler_params=params(56),
        cost_estimate=little(),
        name="leaf",
    )(touched, place, came, stats, leaf_rows, cluster_rows)


def fetches(parts, store_ref, sems):
    step = parts[0].shape[0]
    copies = [
        pltpu.make_async_copy(part, store_ref.at[pl.ds(j * step, step)], sems.at[j])
        for j, part in enumerate(parts)
    ]
    for copy in copies:
        copy.start()
    return copies


def stored(parts):
    step, width = parts[0].shape
    return [pltpu.VMEM((step * len(parts), width), BF), pltpu.SemaphoreType.DMA((len(parts),))]


def in_hbm(count):
    return [pl.BlockSpec(memory_space=pltpu.HBM)] * count


def in_vmem(count):
    return [pl.BlockSpec(memory_space=pltpu.VMEM)] * count


def stat_kernel(*refs):
    parts, users_ref, stat_ref, store_ref, sems = refs[:8], *refs[8:]
    copies = fetches(parts, store_ref, sems)
    step = parts[0].shape[0]
    tiles = 4
    block = users_ref.shape[0] // tiles
    for tile in range(tiles):
        at = pl.ds(tile * block, block)
        users = users_ref[at, :]
        peak = total = None
        for j, copy in enumerate(copies):
            if tile == 0:
                copy.wait()
            rows = store_ref[pl.ds(j * step, step), :]
            score = lax.dot_general(rows, users, NT, preferred_element_type=F32) * LOG2E
            score = score.reshape(step // 8, 8, block)
            high = jnp.max(score, axis=0)
            if peak is None:
                peak = high
                total = jnp.sum(jnp.exp2(score - peak[None]), axis=0)
            else:
                high = jnp.maximum(peak, high)
                total = total * jnp.exp2(peak - high)
                total = total + jnp.sum(jnp.exp2(score - high[None]), axis=0)
                peak = high
        top = jnp.max(peak, axis=0, keepdims=True)
        stat_ref[0:1, at] = top
        stat_ref[1:2, at] = jnp.sum(total * jnp.exp2(peak - top), axis=0, keepdims=True)


def stat_pass(parts, users):
    step, width = parts[0].shape
    clusters, count = step * len(parts), users.shape[0]
    return pl.pallas_call(
        stat_kernel,
        in_specs=in_hbm(8) + in_vmem(1),
        out_shape=jax.ShapeDtypeStruct((2, count), F32),
        scratch_shapes=stored(parts),
        compiler_params=params(24),
        cost_estimate=little(),
        name="stats",
    )(*parts, users)


def user_kernel(*refs):
    parts, users_ref, stat_ref, out_ref, token_ref = refs[:8], *refs[8:12]
    scores, (store_ref, sems) = refs[12:14], refs[14:]
    token_ref[...] = jnp.zeros(token_ref.shape, F32)
    copies = fetches(parts, store_ref, sems)
    step = parts[0].shape[0]
    block = scores[0].shape[0]
    tiles = users_ref.shape[0] // block
    lines = block // LANES

    def score(tile):
        users = users_ref[pl.ds(tile * block, block), :]
        for j, copy in enumerate(copies):
            if tile == 0:
                copy.wait()
            at = pl.ds(j * step, step)
            scores[tile % 2][:, at] = lax.dot_general(
                users, store_ref[at, :], NT, preferred_element_type=F32
            )

    score(0)
    for tile in range(tiles):
        if tile + 1 < tiles:
            score(tile + 1)
        base = tile * block
        peak = jnp.concatenate(
            [
                jnp.broadcast_to(
                    stat_ref[0:1, base + j * LANES : base + (j + 1) * LANES], (LANES, LANES)
                ).T[:, 0:1]
                for j in range(lines)
            ],
            axis=0,
        )
        weight = jnp.exp2(scores[tile % 2][...] * LOG2E - peak).astype(BF)
        out = jnp.dot(weight, store_ref[...], preferred_element_type=F32)
        out_ref[pl.ds(base, block), :] = out.astype(BF)


def user_pass(users, stats, parts):
    count, width = users.shape
    clusters = len(parts) * parts[0].shape[0]
    block = 256
    return pl.pallas_call(
        user_kernel,
        in_specs=in_hbm(8) + in_vmem(2),
        out_shape=[
            jax.ShapeDtypeStruct((count, width), BF),
            jax.ShapeDtypeStruct((8, LANES), F32),
        ],
        scratch_shapes=[pltpu.VMEM((block, clusters), F32)] * 2 + stored(parts),
        compiler_params=params(24),
        cost_estimate=little(),
        name="user_sums",
    )(*parts, users, stats)


def cluster_kernel(place_ref, *refs):
    parts, recv_ref, users_ref = refs[:8], *refs[8:10]
    away_ref, own_ref, factor_ref = refs[11:14]
    scores, (store_ref, sems) = refs[14:16], refs[16:]
    copies = fetches(parts, store_ref, sems)
    peaks = jnp.concatenate([recv_ref[:, j, :] for j in range(8)], axis=1)
    totals = jnp.concatenate([recv_ref[:, 8 + j, :] for j in range(8)], axis=1)
    peak = jnp.max(peaks, axis=0, keepdims=True)
    total = jnp.sum(totals * jnp.exp2(peaks - peak), axis=0, keepdims=True)
    log_row = peak + jnp.log2(total)

    half = place_ref[1] * 2 + (place_ref[2] >> 1)
    mine = recv_ref[:, pl.ds(half, 1), :][:, 0, :]
    for j in range(8):
        @pl.when(half == j)
        def _():
            factor_ref[...] = jnp.exp2(mine - log_row[:, j * 256 : (j + 1) * 256])

    rows = recv_ref.shape[0]
    clusters = own_ref.shape[0]
    for dy in range(4):
        for r in range(2):
            at = clusters + (dy * 2 + r) * rows
            away_ref[pl.ds(at, rows), :] = recv_ref[:, 16 + dy * 4 + 2 + r, :].astype(BF)

    block = parts[0].shape[0]

    def score(j):
        copies[j].wait()
        scores[j % 2][...] = lax.dot_general(
            store_ref[pl.ds(j * block, block), :], users_ref[...], NT, preferred_element_type=F32
        )

    score(0)
    for j in range(len(parts)):
        if j + 1 < len(parts):
            score(j + 1)
        prob = jnp.exp2(scores[j % 2][...] * LOG2E - log_row).astype(BF)
        out = jnp.dot(prob, users_ref[...], preferred_element_type=F32)
        if j < 4:
            away_ref[pl.ds(j * block, block), :] = out.astype(BF)
        else:
            own_ref[pl.ds((j - 4) * block, block), :] = out


def cluster_pass(place, recv, users, far, near, after):
    count, width = users.shape
    parts = far + near
    block = parts[0].shape[0]
    clusters = block * 4
    peers = recv.shape[0]
    return pl.pallas_call(
        cluster_kernel,
        in_specs=[pl.BlockSpec(memory_space=pltpu.SMEM)]
        + in_hbm(8)
        + in_vmem(2)
        + [pl.BlockSpec(memory_space=pl.ANY)],
        out_shape=[
            jax.ShapeDtypeStruct((clusters + 8 * peers, width), BF),
            jax.ShapeDtypeStruct((clusters, width), F32),
            jax.ShapeDtypeStruct((peers, 2 * LANES), F32),
        ],
        scratch_shapes=[pltpu.VMEM((block, count), F32)] * 2 + stored(parts),
        compiler_params=params(28),
        cost_estimate=little(),
        name="cluster_sums",
    )(place, *parts, recv, users, after)


def both_kernel(own_ref, other_ref, recv_ref, out_ref, stay_ref, *sends):
    block = out_ref.shape[0]
    rows = recv_ref.shape[0]
    clusters = own_ref.shape[0]
    out_ref[...] = own_ref[pl.ds(0, block), :] + other_ref[pl.ds(0, block), :].astype(F32)
    for j, send in enumerate(sends):
        at = pl.ds((j + 1) * block, block)
        send[pl.ds(0, block), :] = (own_ref[at, :] + other_ref[at, :].astype(F32)).astype(BF)
    for dy in range(4):
        ref, base = (sends[STEPS.index(4 - dy)], block) if dy else (stay_ref, 0)
        for r in range(2):
            ref[pl.ds(base + r * rows, rows), :] = recv_ref[:, 16 + dy * 4 + r, :].astype(BF)
        ref[pl.ds(base + 2 * rows, 2 * rows), :] = other_ref[
            pl.ds(clusters + dy * 2 * rows, 2 * rows), :
        ]


def both_cores(own, other, recv):
    block, width = own.shape[0] // 4, own.shape[1]
    return pl.pallas_call(
        both_kernel,
        out_shape=[
            jax.ShapeDtypeStruct((block, width), F32),
            jax.ShapeDtypeStruct((64, width), BF),
        ]
        + [jax.ShapeDtypeStruct((block + 64, width), BF)] * 3,
        compiler_params=params(24),
        name="both_cores",
    )(own, other, recv)


def final_kernel(
    touched_ref, place_ref, own_ref, a_ref, b_ref, c_ref, label_ref,
    stay_ref, owner_ref, acc_ref, factor_ref, cluster_ref, user_ref,
):
    block = own_ref.shape[0]
    out = own_ref[...]
    for ref in (a_ref, b_ref, c_ref):
        out = out + ref[pl.ds(0, block), :].astype(F32)
    ids = lax.broadcasted_iota(jnp.int32, out.shape, 0)
    for k in range(2):
        out = out - jnp.where(ids == touched_ref[k], label_ref[k : k + 1, :], 0.0)
    cluster_ref[...] = out

    y, x, z, c = (place_ref[i] for i in range(4))
    users = user_ref.shape[0]
    across = jnp.broadcast_to(owner_ref[...], (users, users))
    rows = lax.broadcasted_iota(jnp.int32, (users, users), 0)
    cols = lax.broadcasted_iota(jnp.int32, (users, users), 1)
    down = jnp.sum(jnp.where(rows == cols, across, 0), axis=1, keepdims=True)
    rank = jnp.sum(((across == down) & (rows < cols)).astype(jnp.int32), axis=0, keepdims=True)
    line = lax.broadcasted_iota(jnp.int32, (256, users), 0)
    target = ((y + (line >> 6)) & 3) * 32 + (line & 15) * 2 + (c ^ ((line >> 5) & 1))
    pick = (target == owner_ref[...]) & (((line >> 4) & 1) == rank)
    pick = pick.astype(F32).astype(BF)
    leaf = jnp.concatenate(
        [stay_ref[...]]
        + [(a_ref, b_ref, c_ref)[ARRIVE.index(4 - dy)][pl.ds(block, 64), :] for dy in (1, 2, 3)],
        axis=0,
    )
    out = lax.dot_general(pick, leaf, TN, preferred_element_type=F32)
    odd = (place_ref[2] & 1) == 1
    factor = jnp.where(odd, factor_ref[:, LANES:], factor_ref[:, :LANES]).T
    for q in range(acc_ref.shape[0]):
        out = out + acc_ref[q].astype(F32) * factor[:, q : q + 1]
    user_ref[...] = out


def final_pass(touched, place, own, arrived, labels, stay, owner, acc, factor):
    return pl.pallas_call(
        final_kernel,
        in_specs=[pl.BlockSpec(memory_space=pltpu.SMEM)] * 2
        + [pl.BlockSpec(memory_space=pltpu.VMEM)] * 9,
        out_shape=[
            jax.ShapeDtypeStruct(own.shape, F32),
            jax.ShapeDtypeStruct(acc.shape[1:], F32),
        ],
        compiler_params=params(24),
        name="final",
    )(touched, place, own, *arrived, labels, stay, owner[None], acc, factor)


def shift(x, axis, by):
    size = lax.axis_size(axis)
    return lax.ppermute(x, axis, [(i, (i + by) % size) for i in range(size)])


def swap(x, axis):
    return lax.all_to_all(x, axis, 0, 0, tiled=True)


def per_device(user_vec, cluster_rows, leaf_rows, touched, route_owner, route_slot, leaf_label):
    peers = lax.axis_size(PLANE)
    count, width = user_vec.shape
    place = jnp.stack([lax.axis_index(name) for name in ALL]).astype(jnp.int32)

    ready = prep(user_vec, route_owner, route_slot, leaf_label)
    near = [cluster_rows] + [shift(cluster_rows, "y", -j) for j in STEPS]
    plane = swap(ready, PLANE)
    far = [shift(part, "c", 1) for part in near]

    users, _, sends = select_pass(place, plane)
    came = swap(sends, ("y", "c"))
    mine = stat_pass(near + far, users)
    back, leaf_grad, labels = leaf_pass(touched, place, came, mine, leaf_rows, cluster_rows)
    recv = swap(back, PLANE)
    acc, token = user_pass(users, mine, near + far)

    away, own, factor = cluster_pass(place, recv, users, far, near, token)
    away = shift(away, "c", 1)
    acc = swap(acc.reshape(peers, count, width), PLANE)
    own, stay, *sends = both_cores(own, away, recv)
    arrived = [shift(sends[STEPS.index(j)], "y", j) for j in ARRIVE]
    cluster_grad, user_grad = final_pass(
        touched, place, own, arrived, labels, stay, route_owner, acc, factor
    )
    return user_grad, cluster_grad, leaf_grad


def solution(mesh):
    grid = Mesh(mesh.devices.reshape(4, 4, 4, 2), ALL)
    one = P(ALL)
    return jax.shard_map(
        per_device,
        mesh=grid,
        in_specs=(P(ALL, None), P(ALL, None), P(ALL, None, None), one, one, one, one),
        out_specs=(P(ALL, None), P(ALL, None), P(ALL, None, None)),
        check_vma=False,
    )
```

```python
import jax
import jax.numpy as jnp
from jax import lax
from jax.experimental import pallas as pl
from jax.experimental.pallas import tpu as pltpu
from jax.sharding import Mesh
from jax.sharding import PartitionSpec as P

BF = jnp.bfloat16
F32 = jnp.float32
LOG2E = 1.4426950408889634
ALL = ("y", "x", "z", "c")
PLANE = ("x", "z")
NT = (((1,), (1,)), ((), ()))
TN = (((0,), (0,)), ((), ()))
META = 128
EXTRA = 16
STEPS = (1, 3, 2)
ARRIVE = (2, 1, 3)
LANES = 128


def params(mib):
    return pltpu.CompilerParams(vmem_limit_bytes=mib << 20)


def little():
    return pl.CostEstimate(flops=1, transcendentals=0, bytes_accessed=1)


def whole(shape):
    return pl.BlockSpec(shape, lambda *ids: (0,) * len(shape))


def prep_kernel(user_ref, owner_ref, slot_ref, leaf_ref, out_ref):
    count, width = user_ref.shape
    for j in range(out_ref.shape[0]):
        out_ref[j, :count, :] = user_ref[...]
    line = lax.broadcasted_iota(jnp.int32, (EXTRA, count), 0)
    leaf = leaf_ref[...]
    left = jnp.where(line == 0, owner_ref[...], jnp.where(line == 1, leaf >> 6, 0))
    right = jnp.where(line == 0, slot_ref[...] + 1, jnp.where(line == 1, leaf & 63, 0))
    both = jnp.concatenate([left, right], axis=1)
    for j in range(out_ref.shape[0]):
        out_ref[j, count:, :] = both.astype(F32).astype(BF)


def prep(user_vec, owner, slot, leaf):
    count, width = user_vec.shape
    return pl.pallas_call(
        prep_kernel,
        out_shape=jax.ShapeDtypeStruct((16, count + EXTRA, width), BF),
        name="prep",
    )(user_vec, owner[None], slot[None], leaf[None])


def select_kernel(place_ref, plane_ref, *refs):
    users_ref, send_ref = refs[:2]
    owner_ref, slot_ref, high_ref, low_ref, rows_ref = refs[2:]
    count = LANES
    width = users_ref.shape[1]
    homes = users_ref.shape[0] // count
    y, x, z, c = (place_ref[i] for i in range(4))
    for home in range(homes):
        users_ref[pl.ds(home * count, count), :] = plane_ref[home, :count, :]
        extra = plane_ref[home, count:, :].astype(F32)
        at = pl.ds(home, 1)
        owner_ref[at, :] = extra[0:1, :count]
        slot_ref[at, :] = extra[0:1, count:]
        high_ref[at, :] = extra[1:2, :count]
        low_ref[at, :] = extra[1:2, count:]

    line = lax.broadcasted_iota(jnp.int32, (8, count), 0)
    target = ((y + (line & 3)) & 3) * 32 + x * 8 + z * 2 + (c ^ (line >> 2))
    target = target.astype(F32)
    match = jnp.concatenate(
        [
            (jnp.broadcast_to(owner_ref[h : h + 1, :], (8, count)) == target).astype(F32)
            for h in range(homes)
        ],
        axis=0,
    )
    rows = lax.broadcasted_iota(jnp.int32, (count, count), 0)
    cols = lax.broadcasted_iota(jnp.int32, (count, count), 1)
    before = (rows < cols).astype(F32).astype(BF)
    rank = jnp.dot(match.astype(BF), before, preferred_element_type=F32)
    first = match * (rank == 0.0).astype(F32)
    second = match * (rank == 1.0).astype(F32)
    lines = lax.broadcasted_iota(jnp.int32, (LANES, count), 0)
    for h in range(homes):
        part = slice(h * 8, (h + 1) * 8)
        pick = jnp.concatenate([first[part], second[part]], axis=0).astype(BF)
        rows_ref[h, :, :width] = jnp.dot(
            pick, users_ref[pl.ds(h * count, count), :], preferred_element_type=F32
        )
        meta = jnp.where(lines == 0, slot_ref[h : h + 1, :], 0.0)
        meta = jnp.where(lines == 1, high_ref[h : h + 1, :], meta)
        meta = jnp.where(lines == 2, low_ref[h : h + 1, :], meta)
        rows_ref[h, :, width:] = lax.dot_general(
            pick, meta.astype(BF), NT, preferred_element_type=F32
        )
    for dy in range(4):
        for core in range(2):
            there = ((y + dy) & 3) * 2 + (c ^ core)
            for r in range(2):
                send_ref[there, pl.ds(r * 16, 16), :] = rows_ref[
                    :, r * 8 + core * 4 + dy, :
                ].astype(BF)


def select_pass(place, plane):
    homes, _, width = plane.shape
    users = homes * LANES
    return pl.pallas_call(
        select_kernel,
        in_specs=[pl.BlockSpec(memory_space=pltpu.SMEM)]
        + [pl.BlockSpec(memory_space=pltpu.VMEM)],
        out_shape=[
            jax.ShapeDtypeStruct((users, width), BF),
            jax.ShapeDtypeStruct((8, 32, width + META), BF),
        ],
        scratch_shapes=[pltpu.VMEM((homes, LANES), F32)] * 4
        + [pltpu.VMEM((homes, 16, width + META), F32)],
        compiler_params=params(16),
        name="select",
    )(place, plane)


def leaf_kernel(*refs):
    touched_ref, place_ref, came_ref, stat_ref, table_ref, cluster_ref = refs[:6]
    back_ref, grad_ref, label_ref, score_ref, recv_ref, part_ref = refs[6:]
    k = pl.program_id(0)
    slots, width = part_ref.shape

    @pl.when(k == 0)
    def _():
        for dy in range(4):
            for core in range(2):
                home = ((place_ref[0] - dy) & 3) * 2 + (place_ref[3] ^ core)
                recv_ref[pl.ds(dy * 64 + core * 32, 32), :] = came_ref[home]

    leaves = table_ref.shape[1]
    step = 512
    users = recv_ref[:, :width]
    meta = recv_ref[:, width:].astype(F32).T
    slot = meta[0:1, :] - 1.0
    leaf = (meta[1:2, :] * 64.0 + meta[2:3, :]).astype(jnp.int32)
    chosen = slot == k.astype(F32)
    leaf = jnp.where(chosen, leaf, -1)

    @pl.when(k == 0)
    def _():
        line = lax.broadcasted_iota(jnp.int32, (16, slots), 0)
        mine = (jnp.broadcast_to(slot, (16, slots)) == line.astype(F32)).astype(F32).astype(BF)
        label_ref[...] = jnp.dot(mine, users, preferred_element_type=F32)
        clusters = cluster_ref.shape[0]
        line = lax.broadcasted_iota(jnp.int32, (16, clusters), 0)
        column = lax.broadcasted_iota(jnp.int32, (16, clusters), 1)
        target = jnp.where(line == 0, touched_ref[0], jnp.where(line == 1, touched_ref[1], -1))
        pick = (column == target).astype(F32).astype(BF)
        rows = jnp.dot(pick, cluster_ref[...], preferred_element_type=F32).astype(BF)
        part_ref[...] = -lax.dot_general(mine, rows, TN, preferred_element_type=F32)

    peak = None
    for j in range(leaves // step):
        score = lax.dot_general(
            table_ref[0, pl.ds(j * step, step), :], users, NT, preferred_element_type=F32
        )
        score_ref[pl.ds(j * step, step), :] = score
        high = jnp.max(score.reshape(step // 8, 8, slots), axis=0)
        peak = high if peak is None else jnp.maximum(peak, high)
    peak = jnp.max(peak, axis=0, keepdims=True) * LOG2E
    total = jnp.zeros((8, slots), F32)
    for j in range(leaves // step):
        weight = jnp.exp2(score_ref[pl.ds(j * step, step), :] * LOG2E - peak)
        score_ref[pl.ds(j * step, step), :] = weight
        total = total + jnp.sum(weight.reshape(step // 8, 8, slots), axis=0)
    scale = chosen.astype(F32) / jnp.sum(total, axis=0, keepdims=True)
    part = jnp.zeros((slots, width), F32)
    for j in range(leaves // step):
        ids = lax.broadcasted_iota(jnp.int32, (step, slots), 0) + j * step
        coef = score_ref[pl.ds(j * step, step), :] * scale - (ids == leaf).astype(F32)
        coef = coef.astype(BF)
        grad_ref[0, pl.ds(j * step, step), :] = jnp.dot(
            coef, users, preferred_element_type=F32
        ).astype(BF)
        part = part + lax.dot_general(
            coef, table_ref[0, pl.ds(j * step, step), :], TN, preferred_element_type=F32
        )
    part_ref[...] += part

    @pl.when(k == pl.num_programs(0) - 1)
    def _():
        peers = back_ref.shape[0]
        for j in range(8):
            at = slice(j * width, (j + 1) * width)
            back_ref[:, j, :] = jnp.broadcast_to(stat_ref[0:1, at], (peers, width))
            back_ref[:, 8 + j, :] = jnp.broadcast_to(stat_ref[1:2, at], (peers, width))
        for j in range(16):
            back_ref[:, 16 + j, :] = part_ref[pl.ds(j * peers, peers), :]


def leaf_pass(touched, place, came, stats, leaf_rows, cluster_rows):
    tables, leaves, width = leaf_rows.shape
    slots = came.shape[0] * came.shape[1]
    peers = slots // 16
    return pl.pallas_call(
        leaf_kernel,
        grid=(tables,),
        in_specs=[
            pl.BlockSpec(memory_space=pltpu.SMEM),
            pl.BlockSpec(memory_space=pltpu.SMEM),
            whole(came.shape),
            whole(stats.shape),
            pl.BlockSpec((1, leaves, width), lambda k: (k, 0, 0)),
            whole(cluster_rows.shape),
        ],
        out_specs=[
            whole((peers, 32, width)),
            pl.BlockSpec((1, leaves, width), lambda k: (k, 0, 0)),
            whole((16, width)),
        ],
        out_shape=[
            jax.ShapeDtypeStruct((peers, 32, width), F32),
            jax.ShapeDtypeStruct(leaf_rows.shape, BF),
            jax.ShapeDtypeStruct((16, width), F32),
        ],
        scratch_shapes=[
            pltpu.VMEM((leaves, slots), F32),
            pltpu.VMEM((slots, width + META), BF),
            pltpu.VMEM((slots, width), F32),
        ],
        compiler_params=params(56),
        cost_estimate=little(),
        name="leaf",
    )(touched, place, came, stats, leaf_rows, cluster_rows)


def fetches(parts, store_ref, sems):
    step = parts[0].shape[0]
    copies = [
        pltpu.make_async_copy(part, store_ref.at[pl.ds(j * step, step)], sems.at[j])
        for j, part in enumerate(parts)
    ]
    for copy in copies:
        copy.start()
    return copies


def stored(parts):
    step, width = parts[0].shape
    return [pltpu.VMEM((step * len(parts), width), BF), pltpu.SemaphoreType.DMA((len(parts),))]


def in_hbm(count):
    return [pl.BlockSpec(memory_space=pltpu.HBM)] * count


def in_vmem(count):
    return [pl.BlockSpec(memory_space=pltpu.VMEM)] * count


def stat_kernel(*refs):
    parts, users_ref, stat_ref, store_ref, sems = refs[:8], *refs[8:]
    copies = fetches(parts, store_ref, sems)
    step = parts[0].shape[0]
    tiles = 4
    block = users_ref.shape[0] // tiles
    for tile in range(tiles):
        at = pl.ds(tile * block, block)
        users = users_ref[at, :]
        peak = total = None
        for j, copy in enumerate(copies):
            if tile == 0:
                copy.wait()
            rows = store_ref[pl.ds(j * step, step), :]
            score = lax.dot_general(rows, users, NT, preferred_element_type=F32) * LOG2E
            score = score.reshape(step // 8, 8, block)
            high = jnp.max(score, axis=0)
            if peak is None:
                peak = high
                total = jnp.sum(jnp.exp2(score - peak[None]), axis=0)
            else:
                high = jnp.maximum(peak, high)
                total = total * jnp.exp2(peak - high)
                total = total + jnp.sum(jnp.exp2(score - high[None]), axis=0)
                peak = high
        top = jnp.max(peak, axis=0, keepdims=True)
        stat_ref[0:1, at] = top
        stat_ref[1:2, at] = jnp.sum(total * jnp.exp2(peak - top), axis=0, keepdims=True)


def stat_pass(parts, users):
    step, width = parts[0].shape
    clusters, count = step * len(parts), users.shape[0]
    return pl.pallas_call(
        stat_kernel,
        in_specs=in_hbm(8) + in_vmem(1),
        out_shape=jax.ShapeDtypeStruct((2, count), F32),
        scratch_shapes=stored(parts),
        compiler_params=params(24),
        cost_estimate=little(),
        name="stats",
    )(*parts, users)


def user_kernel(*refs):
    parts, users_ref, stat_ref, out_ref, token_ref = refs[:8], *refs[8:12]
    scores, (store_ref, sems) = refs[12:14], refs[14:]
    token_ref[...] = jnp.zeros(token_ref.shape, F32)
    copies = fetches(parts, store_ref, sems)
    step = parts[0].shape[0]
    block = scores[0].shape[0]
    tiles = users_ref.shape[0] // block
    lines = block // LANES

    def score(tile):
        users = users_ref[pl.ds(tile * block, block), :]
        for j, copy in enumerate(copies):
            if tile == 0:
                copy.wait()
            at = pl.ds(j * step, step)
            scores[tile % 2][:, at] = lax.dot_general(
                users, store_ref[at, :], NT, preferred_element_type=F32
            )

    score(0)
    for tile in range(tiles):
        if tile + 1 < tiles:
            score(tile + 1)
        base = tile * block
        peak = jnp.concatenate(
            [
                jnp.broadcast_to(
                    stat_ref[0:1, base + j * LANES : base + (j + 1) * LANES], (LANES, LANES)
                ).T[:, 0:1]
                for j in range(lines)
            ],
            axis=0,
        )
        weight = jnp.exp2(scores[tile % 2][...] * LOG2E - peak).astype(BF)
        out = jnp.dot(weight, store_ref[...], preferred_element_type=F32)
        out_ref[pl.ds(base, block), :] = out.astype(BF)


def user_pass(users, stats, parts):
    count, width = users.shape
    clusters = len(parts) * parts[0].shape[0]
    block = 256
    return pl.pallas_call(
        user_kernel,
        in_specs=in_hbm(8) + in_vmem(2),
        out_shape=[
            jax.ShapeDtypeStruct((count, width), BF),
            jax.ShapeDtypeStruct((8, LANES), F32),
        ],
        scratch_shapes=[pltpu.VMEM((block, clusters), F32)] * 2 + stored(parts),
        compiler_params=params(24),
        cost_estimate=little(),
        name="user_sums",
    )(*parts, users, stats)


def cluster_kernel(place_ref, *refs):
    parts, recv_ref, users_ref = refs[:8], *refs[8:10]
    away_ref, own_ref, factor_ref = refs[11:14]
    scores, (store_ref, sems) = refs[14:16], refs[16:]
    copies = fetches(parts, store_ref, sems)
    peaks = jnp.concatenate([recv_ref[:, j, :] for j in range(8)], axis=1)
    totals = jnp.concatenate([recv_ref[:, 8 + j, :] for j in range(8)], axis=1)
    peak = jnp.max(peaks, axis=0, keepdims=True)
    total = jnp.sum(totals * jnp.exp2(peaks - peak), axis=0, keepdims=True)
    log_row = peak + jnp.log2(total)

    half = place_ref[1] * 2 + (place_ref[2] >> 1)
    mine = recv_ref[:, pl.ds(half, 1), :][:, 0, :]
    for j in range(8):
        @pl.when(half == j)
        def _():
            factor_ref[...] = jnp.exp2(mine - log_row[:, j * 256 : (j + 1) * 256])

    rows = recv_ref.shape[0]
    clusters = own_ref.shape[0]
    for dy in range(4):
        for r in range(2):
            at = clusters + (dy * 2 + r) * rows
            away_ref[pl.ds(at, rows), :] = recv_ref[:, 16 + dy * 4 + 2 + r, :].astype(BF)

    block = parts[0].shape[0]

    def score(j):
        copies[j].wait()
        scores[j % 2][...] = lax.dot_general(
            store_ref[pl.ds(j * block, block), :], users_ref[...], NT, preferred_element_type=F32
        )

    score(0)
    for j in range(len(parts)):
        if j + 1 < len(parts):
            score(j + 1)
        prob = jnp.exp2(scores[j % 2][...] * LOG2E - log_row).astype(BF)
        out = jnp.dot(prob, users_ref[...], preferred_element_type=F32)
        if j < 4:
            away_ref[pl.ds(j * block, block), :] = out.astype(BF)
        else:
            own_ref[pl.ds((j - 4) * block, block), :] = out.astype(BF)


def cluster_pass(place, recv, users, far, near, after):
    count, width = users.shape
    parts = far + near
    block = parts[0].shape[0]
    clusters = block * 4
    peers = recv.shape[0]
    return pl.pallas_call(
        cluster_kernel,
        in_specs=[pl.BlockSpec(memory_space=pltpu.SMEM)]
        + in_hbm(8)
        + in_vmem(2)
        + [pl.BlockSpec(memory_space=pl.ANY)],
        out_shape=[
            jax.ShapeDtypeStruct((clusters + 8 * peers, width), BF),
            jax.ShapeDtypeStruct((clusters, width), BF),
            jax.ShapeDtypeStruct((peers, 2 * LANES), F32),
        ],
        scratch_shapes=[pltpu.VMEM((block, count), F32)] * 2 + stored(parts),
        compiler_params=params(28),
        cost_estimate=little(),
        name="cluster_sums",
    )(place, *parts, recv, users, after)


def both_kernel(own_ref, other_ref, recv_ref, out_ref, stay_ref, *sends):
    block = out_ref.shape[0]
    rows = recv_ref.shape[0]
    clusters = own_ref.shape[0]
    out_ref[...] = own_ref[pl.ds(0, block), :].astype(F32) + other_ref[pl.ds(0, block), :].astype(F32)
    for j, send in enumerate(sends):
        at = pl.ds((j + 1) * block, block)
        send[pl.ds(0, block), :] = (own_ref[at, :].astype(F32) + other_ref[at, :].astype(F32)).astype(BF)
    for dy in range(4):
        ref, base = (sends[STEPS.index(4 - dy)], block) if dy else (stay_ref, 0)
        for r in range(2):
            ref[pl.ds(base + r * rows, rows), :] = recv_ref[:, 16 + dy * 4 + r, :].astype(BF)
        ref[pl.ds(base + 2 * rows, 2 * rows), :] = other_ref[
            pl.ds(clusters + dy * 2 * rows, 2 * rows), :
        ]


def both_cores(own, other, recv):
    block, width = own.shape[0] // 4, own.shape[1]
    return pl.pallas_call(
        both_kernel,
        out_shape=[
            jax.ShapeDtypeStruct((block, width), F32),
            jax.ShapeDtypeStruct((64, width), BF),
        ]
        + [jax.ShapeDtypeStruct((block + 64, width), BF)] * 3,
        compiler_params=params(24),
        name="both_cores",
    )(own, other, recv)


def final_kernel(
    touched_ref, place_ref, own_ref, a_ref, b_ref, c_ref, label_ref,
    stay_ref, owner_ref, acc_ref, factor_ref, cluster_ref, user_ref,
):
    block = own_ref.shape[0]
    out = own_ref[...]
    for ref in (a_ref, b_ref, c_ref):
        out = out + ref[pl.ds(0, block), :].astype(F32)
    ids = lax.broadcasted_iota(jnp.int32, out.shape, 0)
    for k in range(2):
        out = out - jnp.where(ids == touched_ref[k], label_ref[k : k + 1, :], 0.0)
    cluster_ref[...] = out

    y, x, z, c = (place_ref[i] for i in range(4))
    users = user_ref.shape[0]
    across = jnp.broadcast_to(owner_ref[...], (users, users))
    rows = lax.broadcasted_iota(jnp.int32, (users, users), 0)
    cols = lax.broadcasted_iota(jnp.int32, (users, users), 1)
    down = jnp.sum(jnp.where(rows == cols, across, 0), axis=1, keepdims=True)
    rank = jnp.sum(((across == down) & (rows < cols)).astype(jnp.int32), axis=0, keepdims=True)
    line = lax.broadcasted_iota(jnp.int32, (256, users), 0)
    target = ((y + (line >> 6)) & 3) * 32 + (line & 15) * 2 + (c ^ ((line >> 5) & 1))
    pick = (target == owner_ref[...]) & (((line >> 4) & 1) == rank)
    pick = pick.astype(F32).astype(BF)
    leaf = jnp.concatenate(
        [stay_ref[...]]
        + [(a_ref, b_ref, c_ref)[ARRIVE.index(4 - dy)][pl.ds(block, 64), :] for dy in (1, 2, 3)],
        axis=0,
    )
    out = lax.dot_general(pick, leaf, TN, preferred_element_type=F32)
    odd = (place_ref[2] & 1) == 1
    factor = jnp.where(odd, factor_ref[:, LANES:], factor_ref[:, :LANES]).T
    for q in range(acc_ref.shape[0]):
        out = out + acc_ref[q].astype(F32) * factor[:, q : q + 1]
    user_ref[...] = out


def final_pass(touched, place, own, arrived, labels, stay, owner, acc, factor):
    return pl.pallas_call(
        final_kernel,
        in_specs=[pl.BlockSpec(memory_space=pltpu.SMEM)] * 2
        + [pl.BlockSpec(memory_space=pltpu.VMEM)] * 9,
        out_shape=[
            jax.ShapeDtypeStruct(own.shape, F32),
            jax.ShapeDtypeStruct(acc.shape[1:], F32),
        ],
        compiler_params=params(24),
        name="final",
    )(touched, place, own, *arrived, labels, stay, owner[None], acc, factor)


def shift(x, axis, by):
    size = lax.axis_size(axis)
    return lax.ppermute(x, axis, [(i, (i + by) % size) for i in range(size)])


def swap(x, axis):
    return lax.all_to_all(x, axis, 0, 0, tiled=True)


def per_device(user_vec, cluster_rows, leaf_rows, touched, route_owner, route_slot, leaf_label):
    peers = lax.axis_size(PLANE)
    count, width = user_vec.shape
    place = jnp.stack([lax.axis_index(name) for name in ALL]).astype(jnp.int32)

    ready = prep(user_vec, route_owner, route_slot, leaf_label)
    near = [cluster_rows] + [shift(cluster_rows, "y", -j) for j in STEPS]
    plane = swap(ready, PLANE)
    far = [shift(part, "c", 1) for part in near]

    users, sends = select_pass(place, plane)
    came = swap(sends, ("y", "c"))
    mine = stat_pass(near + far, users)
    back, leaf_grad, labels = leaf_pass(touched, place, came, mine, leaf_rows, cluster_rows)
    recv = swap(back, PLANE)
    acc, token = user_pass(users, mine, near + far)

    away, own, factor = cluster_pass(place, recv, users, far, near, token)
    away = shift(away, "c", 1)
    acc = swap(acc.reshape(peers, count, width), PLANE)
    own, stay, *sends = both_cores(own, away, recv)
    arrived = [shift(sends[STEPS.index(j)], "y", j) for j in ARRIVE]
    cluster_grad, user_grad = final_pass(
        touched, place, own, arrived, labels, stay, route_owner, acc, factor
    )
    return user_grad, cluster_grad, leaf_grad


def solution(mesh):
    grid = Mesh(mesh.devices.reshape(4, 4, 4, 2), ALL)
    one = P(ALL)
    return jax.shard_map(
        per_device,
        mesh=grid,
        in_specs=(P(ALL, None), P(ALL, None), P(ALL, None, None), one, one, one, one),
        out_specs=(P(ALL, None), P(ALL, None), P(ALL, None, None)),
        check_vma=False,
    )
```
